512 devices in a mesh: bead: 8 (over x_hi, y), space: 64 (over z, x_lo, core).
Axes of the slice: x: 4 (x_hi: 2, x_lo: 2; x = x_hi * 2 + x_lo), y: 4, z: 16, core: 2. Of those that a mesh axis runs over, the one named last changes fastest.
Arguments:
- positions: float32 [8, 3, 16384], P('bead', None, 'space'), may hold values from 0 to 3
- momenta: float32 [8, 3, 16384], P('bead', None, 'space'), may hold values from -6 to 6
- species: int32 [16384], P('space'), may hold values 0 or 1
- neighbours: int32 [16384, 24], P('space'), may hold values from 0 to 384, as said below
- send_low: int32 [4096], P('space'), may hold values from 0 to 255, as said below
- send_high: int32 [4096], P('space'), may hold values from 0 to 255, as said below
- species_embed: float32 [2, 128], replicated, may hold values from -6 to 6
- w_radial_in: float32 [2, 8, 64], replicated, may hold values from -12 to 12
- w_radial_out: bfloat16 [2, 64, 128], replicated, may hold values from -1.5 to 1.5
- w_message: bfloat16 [2, 128, 128], replicated, may hold values from -0.5 to 0.5
- w_update: bfloat16 [2, 128, 128], replicated, may hold values from -0.5 to 0.5
- w_energy: float32 [128], replicated, may hold values from -3 to 3
Outputs:
- new_positions: float32 [8, 3, 16384], P('bead', None, 'space')
- new_momenta: float32 [8, 3, 16384], P('bead', None, 'space')
- forces: float32 [8, 3, 16384], P('bead', None, 'space')
The draws below stay inside these ranges and needn't reach their ends.
Inputs may be any that keep to these rules, and one draw needn't show every extreme that they name: `neighbours`: entry k of row i names a neighbour of local atom i of the same brick: below 256 a local atom, 256 + m the atom named by entry m of the lower brick's send_high, 320 + m the atom named by entry m of the upper brick's send_low, 384 an empty slot at no fixed place; the atoms of a row are distinct and never the atom itself, and each row has 6 or more of them. `send_low`: the 64 entries of one brick are distinct local atom numbers, none of them in that brick's send_high. `send_high`: the 64 entries of one brick are distinct local atom numbers.
All inputs are finite; a program needn't handle non-finite values. No bound on the sum of `species` on one device may be relied on, other than what follows from the above.
Results may differ from the reference program's by a relative error of at most 0.025.
Values may be sent and summed in bfloat16 or wider, within the bound.
A program may use at most 64 MiB of HBM per device.

```python
import jax
import jax.numpy as jnp
from jax import lax

C = 128
RH = 64
NB = 8
K = 24
A = 256
G = 64
BEADS = 8
SLABS = 64
ATOMS = 16384


def neighbour_tables(key):
    slab_keys = jax.random.split(jax.random.fold_in(key, 11), SLABS)
    slot_of_rank = jax.vmap(lambda one_key: jax.random.permutation(one_key, A))(slab_keys).astype(jnp.int32)
    slab_rows = jnp.arange(SLABS)[:, None]
    rank_of_slot = jnp.zeros((SLABS, A), jnp.int32).at[slab_rows, slot_of_rank].set(jnp.broadcast_to(jnp.arange(A).astype(jnp.int32), (SLABS, A)))
    window_size = 2 * G // K
    jitter = jax.random.randint(jax.random.fold_in(key, 12), (SLABS, A, K), 0, window_size)
    offsets = -G + jnp.arange(K)[None, None, :] * window_size + jitter
    offsets = offsets + (offsets >= 0).astype(jnp.int32)
    rotation = jax.random.randint(jax.random.fold_in(key, 13), (SLABS, A, 1), 0, K)
    offsets = jnp.take_along_axis(offsets, (jnp.arange(K)[None, None, :] + rotation) % K, axis=2)
    spans = jax.random.randint(jax.random.fold_in(key, 14), (SLABS, 1), 2, 3 * K // 4 + 1)
    counts = K - jax.random.randint(jax.random.fold_in(key, 15), (SLABS, A), 0, spans)
    counts = counts.at[:, 0].set(K // 4)
    live_mask = jnp.arange(K)[None, None, :] < counts[:, :, None]
    target = rank_of_slot[:, :, None] + offsets
    inside = jnp.take_along_axis(slot_of_rank, jnp.clip(target, 0, A - 1).reshape(SLABS, -1), axis=1).reshape(SLABS, A, K)
    ext_index = jnp.where(target < 0, A + G + target, jnp.where(target >= A, G + target, inside))
    ext_index = jnp.where(live_mask, ext_index, A + 2 * G)
    send_lower = slot_of_rank[:, :G].reshape(-1)
    send_upper = slot_of_rank[:, A - G:].reshape(-1)
    return (ext_index.reshape(SLABS * A, K).astype(jnp.int32), send_lower.astype(jnp.int32), send_upper.astype(jnp.int32))


def draw_neighbours(key, part):
    return neighbour_tables(key)[0]


def draw_send_low(key, part):
    return neighbour_tables(key)[1]


def draw_send_high(key, part):
    return neighbour_tables(key)[2]


def place_ends(values, own_key, smallest, largest):
    index_at = [jax.random.randint(jax.random.fold_in(own_key, axis), (), 0, length) for axis, length in enumerate(values.shape)]
    longest = values.shape.index(max(values.shape))
    neighbour = index_at[:longest] + [(index_at[longest] + 1) % values.shape[longest]] + index_at[longest + 1:]
    return values.at[tuple(index_at)].set(smallest).at[tuple(neighbour)].set(largest)


def shard_levels(rng, shape, cuts, least, largest):
    def one(dim, blocks):
        draws = jax.random.uniform(jax.random.fold_in(jax.random.fold_in(rng, 6), dim), (blocks,), jnp.float32, least / len(cuts), largest / len(cuts))
        return jnp.repeat(jnp.exp(draws), shape[dim] // blocks).reshape((-1,) + (1,) * (len(shape) - dim - 1))

    loudness = one(*cuts[0])
    for cut in cuts[1:]:
        loudness = loudness * one(*cut)
    return loudness


def normal_values(rng, dims, width, limit, cuts=(), kind=jnp.bfloat16):
    values = width * jax.random.normal(rng, dims, jnp.float32)
    if cuts:
        values = values * shard_levels(rng, dims, cuts, -0.22, 0.18)
    return jnp.clip(values, -limit, limit).astype(kind)


def setup_inputs(seed: int = 0) -> dict:
    key_of = jax.random.split(jax.random.key(seed), 13)
    return {
        "positions": jnp.clip(3.0 * jax.random.uniform(key_of[0], (BEADS, 3, ATOMS), jnp.float32) ** shard_levels(key_of[0], (BEADS, 3, ATOMS), ((0, 8), (2, 64)), -0.2, 0.2), 0.0, 3.0),
        "momenta": normal_values(key_of[1], (BEADS, 3, ATOMS), 1.0, 6.0, ((0, 8), (2, 64)), jnp.float32),
        "species": place_ends((jax.random.randint(key_of[2], (ATOMS,), 0, 3) < 1).astype(jnp.int32), jax.random.fold_in(key_of[2], 1), 0, 1),
        "neighbours": draw_neighbours(jax.random.fold_in(key_of[12], 71), 0),
        "send_low": draw_send_low(jax.random.fold_in(key_of[12], 71), 0),
        "send_high": draw_send_high(jax.random.fold_in(key_of[12], 71), 0),
        "species_embed": normal_values(key_of[6], (2, C), 1.0, 6.0, (), jnp.float32),
        "w_radial_in": normal_values(key_of[7], (2, NB, RH), 2.0, 12.0, (), jnp.float32),
        "w_radial_out": normal_values(key_of[8], (2, RH, C), (RH // 4) ** -0.5, 1.5),
        "w_message": normal_values(key_of[9], (2, C, C), C ** -0.5, 0.5),
        "w_update": normal_values(key_of[10], (2, C, C), C ** -0.5, 0.5),
        "w_energy": normal_values(key_of[11], (C,), 0.5, 3.0, (), jnp.float32),
    }


cutoff_radius = 8.0
slab_width = 3.0
soft_square = 0.25
time_step = 0.5
cycle_angle = 2.0
light_mass = 1.0
heavy_mass = 16.0
highest = lax.Precision.HIGHEST

def radial_basis(distance, basis_count):
    orders = jnp.arange(1, basis_count + 1).astype(jnp.float32)
    scaled = distance / cutoff_radius
    envelope = (1.0 - scaled * scaled) ** 2
    waves = jnp.sin(jnp.pi * orders[:, None] * scaled[None, :])
    return waves * (envelope / distance)[None, :]

def block_messages(centres, ext_positions, block_nbr, sources, w_in, w_out):
    ext_count = ext_positions.shape[1]
    row_count, slot_count = block_nbr.shape
    flat_index = block_nbr.reshape(-1)
    live_mask = (flat_index < ext_count).astype(jnp.float32)
    safe_index = jnp.minimum(flat_index, ext_count - 1)
    others = ext_positions[:, safe_index].reshape(3, row_count, slot_count)
    separation = (others - centres[:, :, None]).reshape(3, -1)
    distance = jnp.sqrt(lax.optimization_barrier(jnp.sum(separation * separation, axis=0)) + soft_square)
    basis_rows = radial_basis(distance, w_in.shape[0])
    hidden = jax.nn.silu(jnp.dot(w_in.T, basis_rows, precision=highest)).astype(jnp.bfloat16)
    radial = lax.dot_general(hidden, w_out, (((0,), (0,)), ((), ())), preferred_element_type=jnp.float32)
    gathered = sources[safe_index]
    terms = radial * gathered.astype(jnp.float32) * live_mask[:, None]
    return lax.optimization_barrier(jnp.sum(terms.reshape(row_count, slot_count, -1), axis=1)) / jnp.sqrt(float(slot_count))

def all_messages(ext_positions, nbr_rows, sources, w_in, w_out):
    atom_count = nbr_rows.shape[0]
    block_rows = min(256, atom_count)
    block_count = atom_count // block_rows
    centres = ext_positions[:, :atom_count].reshape(3, block_count, block_rows).transpose(1, 0, 2)
    nbr_blocks = nbr_rows.reshape(block_count, block_rows, -1)
    block_fn = jax.checkpoint(lambda cen_rows, nbr_part: block_messages(cen_rows, ext_positions, nbr_part, sources, w_in, w_out))
    result = lax.map(lambda pair_in: block_fn(pair_in[0], pair_in[1]), (centres, nbr_blocks))
    return result.reshape(atom_count, -1)

def interaction(ext_features, ext_positions, nbr_rows, w_in, w_out, w_msg, w_upd):
    atom_count = nbr_rows.shape[0]
    sources = jnp.dot(ext_features.astype(jnp.bfloat16), w_msg, preferred_element_type=jnp.float32).astype(jnp.bfloat16)
    messages = all_messages(ext_positions, nbr_rows, sources, w_in, w_out).astype(jnp.bfloat16)
    update = jnp.dot(messages, w_upd, preferred_element_type=jnp.float32)
    return ext_features[:atom_count] + jax.nn.silu(update)

def mode_tables(bead_count):
    bead_index = jnp.arange(bead_count).astype(jnp.float32)
    phase_grid = 2.0 * jnp.pi * bead_index[:, None] * bead_index[None, :] / bead_count
    mode_ids = jnp.arange(bead_count)[None, :]
    half_count = bead_count // 2
    scale_one = 1.0 / jnp.sqrt(float(bead_count))
    scale_two = jnp.sqrt(2.0 / bead_count)
    mode_table = jnp.where(mode_ids == 0, scale_one + 0.0 * phase_grid, jnp.where(mode_ids < half_count, scale_two * jnp.cos(phase_grid), jnp.where(mode_ids == half_count, scale_one * jnp.cos(phase_grid), scale_two * jnp.sin(phase_grid))))
    mode_angle = 2.0 * cycle_angle * jnp.sin(jnp.pi * bead_index / bead_count)
    nonzero = jnp.arange(bead_count) > 0
    safe_angle = jnp.where(nonzero, mode_angle, 1.0)
    sinc_value = jnp.where(nonzero, jnp.sin(mode_angle) / safe_angle, 1.0)
    return (mode_table.astype(jnp.float32), jnp.cos(mode_angle), time_step * sinc_value, mode_angle * jnp.sin(mode_angle) / time_step)

def reference(positions, momenta, species, neighbours, send_low, send_high, species_embed, w_radial_in, w_radial_out, w_message, w_update, w_energy):
    bead_count = positions.shape[0]
    low_lists = send_low.reshape(SLABS, G)
    high_lists = send_high.reshape(SLABS, G)
    slab_ids = jnp.arange(SLABS).astype(jnp.int32)
    before = (slab_ids - 1) % SLABS
    after = (slab_ids + 1) % SLABS
    ext_index = jnp.concatenate([slab_ids[:, None] * A + jnp.arange(A).astype(jnp.int32)[None, :], before[:, None] * A + high_lists[before], after[:, None] * A + low_lists[after]], axis=1).astype(jnp.int32)
    z_shift = jnp.concatenate([jnp.zeros((A,), jnp.float32), jnp.full((G,), -slab_width, jnp.float32), jnp.full((G,), slab_width, jnp.float32)])
    nbr_slabs = neighbours.reshape(SLABS, A, K)
    embedded_all = species_embed[species]
    item_count = bead_count * SLABS
    bead_of = (jnp.arange(item_count) // SLABS).astype(jnp.int32)
    slab_of = (jnp.arange(item_count) % SLABS).astype(jnp.int32)

    def total_energy(coords):

        def ext_of(bead_id, slab_id):
            ext_positions = coords[bead_id][:, ext_index[slab_id]]
            return ext_positions.at[2].add(z_shift)

        def first_item(work_item):
            bead_id, slab_id = work_item
            ext_positions = ext_of(bead_id, slab_id)
            return interaction(embedded_all[ext_index[slab_id]], ext_positions, nbr_slabs[slab_id], w_radial_in[0], w_radial_out[0], w_message[0], w_update[0])
        layer_one = lax.map(jax.checkpoint(first_item), (bead_of, slab_of)).reshape(bead_count, SLABS * A, -1)

        def second_item(work_item):
            bead_id, slab_id = work_item
            ext_positions = ext_of(bead_id, slab_id)
            layer_two = interaction(layer_one[bead_id][ext_index[slab_id]], ext_positions, nbr_slabs[slab_id], w_radial_in[1], w_radial_out[1], w_message[1], w_update[1])
            return jnp.sum(jnp.dot(layer_two, w_energy, precision=highest))
        return jnp.sum(lax.map(jax.checkpoint(second_item), (bead_of, slab_of)))
    forces = -jax.grad(total_energy)(positions)
    atom_mass = jnp.where(species == 1, heavy_mass, light_mass).astype(jnp.float32)
    half_kick = momenta + 0.5 * time_step * forces
    mode_table, cosine, reach, pull = mode_tables(bead_count)
    modes_q = jnp.einsum('bk,bcn->kcn', mode_table, positions, precision=highest)
    modes_p = jnp.einsum('bk,bcn->kcn', mode_table, half_kick, precision=highest)
    turned_q = cosine[:, None, None] * modes_q + reach[:, None, None] * modes_p / atom_mass
    turned_p = cosine[:, None, None] * modes_p - pull[:, None, None] * atom_mass * modes_q
    new_positions = jnp.einsum('bk,kcn->bcn', mode_table, turned_q, precision=highest)
    new_momenta = jnp.einsum('bk,kcn->bcn', mode_table, turned_p, precision=highest)
    return (new_positions, new_momenta, forces)
```

```python
import functools

import jax
import jax.numpy as jnp
import numpy as np
from jax import lax
from jax.experimental import pallas as pl
from jax.experimental.pallas import tpu as pltpu
from jax.sharding import PartitionSpec as P

cutoff_radius = 8.0
slab_width = 3.0
soft_square = 0.25
time_step = 0.5
cycle_angle = 2.0
light_mass = 1.0
heavy_mass = 16.0

ATOMS = 256
FACES = 64
SLOTS = 24
CH = 128
HID = 64
GROUP = 4
LANES = GROUP * ATOMS
STEPS = SLOTS // GROUP
EDGES = SLOTS * ATOMS
EXT = ATOMS + 2 * FACES

f32 = jnp.float32
bf16 = jnp.bfloat16
NT = (((1,), (1,)), ((), ()))


def mm(a, b):
    return jnp.dot(a, b, preferred_element_type=f32)


def mm_nt(a, b):
    return lax.dot_general(a, b, NT, preferred_element_type=f32)


def split_rows(x):
    hi = x.astype(bf16).astype(f32)
    mid = (x - hi).astype(bf16).astype(f32)
    low = x - hi - mid
    return jnp.concatenate([hi, mid, low, jnp.zeros_like(x)], axis=0).astype(bf16)


def join_rows(y):
    return y[0:8] + y[8:16] + y[16:24]


def tile(a):
    return jnp.concatenate([a] * GROUP, axis=1)


def fold(a):
    total = a[:, :ATOMS]
    for u in range(1, GROUP):
        total = total + a[:, u * ATOMS : (u + 1) * ATOMS]
    return total


def sigmoid(x):
    return 0.5 * jnp.tanh(0.5 * x) + 0.5


def sin_pi(z, zz):
    acc = -np.pi**11 / 39916800.0
    for c in (np.pi**9 / 362880.0, -np.pi**7 / 5040.0, np.pi**5 / 120.0, -np.pi**3 / 6.0, np.pi):
        acc = acc * zz + float(c)
    return acc * z


def cos_pi(zz):
    acc = np.pi**12 / 479001600.0
    for c in (
        -np.pi**10 / 3628800.0,
        np.pi**8 / 40320.0,
        -np.pi**6 / 720.0,
        np.pi**4 / 24.0,
        -np.pi**2 / 2.0,
        1.0,
    ):
        acc = acc * zz + float(c)
    return acc


def mode_mix(bead_count):
    k = np.arange(bead_count)
    angle = 2.0 * cycle_angle * np.sin(np.pi * k / bead_count)
    sinc = np.where(k > 0, np.sin(angle) / np.where(k > 0, angle, 1.0), 1.0)
    weights = (np.cos(angle), time_step * sinc, -angle * np.sin(angle) / time_step)
    gap = np.cos(2.0 * np.pi * k[:, None] * k[None, :] / bead_count) / bead_count
    return [[float(v) for v in gap @ w] for w in weights]


def kernel(
    beads,
    slabs,
    pos_ref,
    mom_ref,
    spec_ref,
    nbr_ref,
    low_ref,
    high_ref,
    emb_ref,
    win_ref,
    wout_ref,
    wmsg_ref,
    wupd_ref,
    wen_ref,
    newq_ref,
    newp_ref,
    force_ref,
    pos8,
    small8,
    win32,
    hot,
    ext32,
    basis_buf,
    slope_buf,
    unit_buf,
    mask_buf,
    d0_buf,
    d1_buf,
    rad_buf,
    gat_buf,
    dt_buf,
    db_buf,
    f_buf,
    hsum,
    msum,
    ghost_sum,
    fghost,
    send_a,
    recv_a,
    send_b,
    recv_b,
    send_c,
    recv_c,
    send_d,
    recv_d,
    q_all,
    p_all,
    halo_send,
    halo_recv,
    bead_send,
    bead_recv,
):
    bead = lax.axis_index("bead")
    slab = lax.axis_index("space")
    left = lax.rem(slab + slabs - 1, slabs)
    right = lax.rem(slab + 1, slabs)

    def halo(n, src, dst, target):
        return pltpu.make_async_remote_copy(
            src_ref=src,
            dst_ref=dst,
            send_sem=halo_send.at[n],
            recv_sem=halo_recv.at[n],
            device_id=(bead, target),
            device_id_type=pl.DeviceIdType.MESH,
        )

    def to_bead(n, buf, gap):
        return pltpu.make_async_remote_copy(
            src_ref=buf.at[0],
            dst_ref=buf.at[beads - gap],
            send_sem=bead_send.at[n * beads + gap],
            recv_sem=bead_recv.at[n * beads + beads - gap],
            device_id=(lax.rem(bead + gap, beads), slab),
            device_id_type=pl.DeviceIdType.MESH,
        )

    barrier = pltpu.get_barrier_semaphore()
    for target in (left, right):
        pl.semaphore_signal(
            barrier, inc=1, device_id=(bead, target), device_id_type=pl.DeviceIdType.MESH
        )
    for gap in range(1, beads):
        pl.semaphore_signal(
            barrier,
            inc=1,
            device_id=(lax.rem(bead + gap, beads), slab),
            device_id_type=pl.DeviceIdType.MESH,
        )

    heavy = (spec_ref[...] == 1).astype(f32)
    pos8[...] = jnp.zeros_like(pos8)
    for c in range(3):
        pos8[c : c + 1, :] = pos_ref[c]
    own8 = pos8[...]
    q_all[0] = own8
    row8 = lax.broadcasted_iota(jnp.int32, (8, ATOMS), 0)
    code8 = own8 + jnp.where(row8 == 3, heavy, 0.0) + jnp.where(row8 == 4, 1.0, 0.0)

    face_row = jnp.concatenate([high_ref[...], low_ref[...]], axis=1)
    face_t = jnp.where(
        lax.broadcasted_iota(jnp.int32, (ATOMS, 2 * FACES), 0) == face_row, 1.0, 0.0
    )
    face_hot_t = face_t.astype(bf16)
    face_hot = face_t.T.astype(bf16)
    own32 = split_rows(code8)
    send_a[...] = join_rows(mm(own32, face_hot_t))

    pl.semaphore_wait(barrier, beads + 1)
    a_right = halo(0, send_a, recv_a.at[0], right)
    a_left = halo(1, send_a, recv_a.at[1], left)
    a_right.start()
    a_left.start()
    q_copies = [to_bead(0, q_all, gap) for gap in range(1, beads)]
    for copy in q_copies:
        copy.start()

    ext_iota = lax.broadcasted_iota(jnp.int32, (EXT, ATOMS), 0)

    def build(step, carry):
        for u in range(GROUP):
            slot = step * GROUP + u
            row = nbr_ref[pl.ds(slot, 1), :]
            hot[:, pl.ds(pl.multiple_of(slot * ATOMS, ATOMS), ATOMS)] = jnp.where(
                ext_iota == row, 1.0, 0.0
            ).astype(bf16)
        return carry

    lax.fori_loop(0, STEPS, build, 0)

    w8 = jnp.concatenate([win_ref[0], win_ref[1]], axis=1)
    w8_hi = w8.astype(bf16).astype(f32)
    w8_low = w8 - w8_hi
    win32[...] = jnp.zeros_like(win32)
    win32[0:8, :] = w8_hi
    win32[8:16, :] = w8_hi
    win32[16:24, :] = w8_low
    w_in_t = win32[...].T[:, :32].astype(bf16)
    w_in_b = jnp.concatenate([w8_hi, w8_low], axis=0).astype(bf16)
    small8[...] = jnp.zeros_like(small8)
    small8[0:2, :] = emb_ref[...]
    small8[2:3, :] = wen_ref[...]
    columns = small8[...].T
    light_col, heavy_col, energy_col = columns[:, 0:1], columns[:, 1:2], columns[:, 2:3]
    kinds = mm(small8[0:8, :].astype(bf16), wmsg_ref[0]).astype(bf16).astype(f32)
    w_out0 = wout_ref[0].astype(f32)
    pair_out = jnp.concatenate([w_out0 * kinds[0:1, :], w_out0 * kinds[1:2, :]], axis=0)
    pair_out_t = pair_out.T.astype(bf16)
    pair_out = pair_out.astype(bf16)
    w_out1 = wout_ref[1]
    w_out1_t = w_out1.astype(f32).T.astype(bf16)
    w_upd0_t = wupd_ref[0].astype(f32).T.astype(bf16)
    w_upd1_t = wupd_ref[1].astype(f32).T.astype(bf16)
    w_msg1_t = wmsg_ref[1].astype(f32).T.astype(bf16)
    scale = float(1.0 / np.sqrt(SLOTS))

    a_right.wait_recv()
    a_left.wait_recv()
    row_g = lax.broadcasted_iota(jnp.int32, (8, 2 * FACES), 0)
    lane_g = lax.broadcasted_iota(jnp.int32, (8, 2 * FACES), 1)
    shift = jnp.where(row_g == 2, jnp.where(lane_g < FACES, -slab_width, slab_width), 0.0)
    ghost8 = jnp.where(lane_g < FACES, recv_a[0], recv_a[1]) + shift
    ext32[:, :ATOMS] = own32
    ext32[:, ATOMS:] = split_rows(ghost8)

    orders = lax.broadcasted_iota(jnp.int32, (8, LANES), 0).astype(f32) + 1.0
    is_xyz = lax.broadcasted_iota(jnp.int32, (8, LANES), 0) < 3

    hsum[...] = jnp.zeros_like(hsum)

    def geometry(step, carry):
        cols = pl.ds(pl.multiple_of(step * LANES, LANES), LANES)
        found = join_rows(mm(ext32[...], hot[:, cols]))
        mask_buf[:, cols] = found
        away = jnp.where(is_xyz, found - tile(own8), 0.0)
        square = jnp.sum(away * away, axis=0, keepdims=True) + soft_square
        inverse = lax.rsqrt(square)
        scaled = square * inverse * (1.0 / cutoff_radius)
        unit_buf[:, cols] = away * inverse
        phase = orders * scaled
        whole = jnp.floor(phase + 0.5)
        z = phase - whole
        sign = 1.0 - 2.0 * (whole - 2.0 * jnp.floor(whole * 0.5))
        zz = z * z
        sine = sign * sin_pi(z, zz)
        cosine = sign * cos_pi(zz)
        rest = 1.0 - scaled * scaled
        ratio = rest * rest * inverse
        ratio_slope = -(0.5 * scaled * rest + ratio) * inverse
        waves = sine * ratio
        slope_buf[:, cols] = cosine * (orders * (ratio * (np.pi / cutoff_radius))) + (
            sine * ratio_slope
        )
        waves_hi = waves.astype(bf16).astype(f32)
        stack = jnp.concatenate(
            [waves_hi, waves - waves_hi, waves_hi, jnp.zeros_like(waves)], axis=0
        ).astype(bf16)
        basis_buf[:, cols] = stack
        pre = mm(w_in_t[:HID], stack)
        gate = sigmoid(pre)
        act = pre * gate
        d0_buf[:, cols] = (gate + act * (1.0 - gate)).astype(bf16)
        act = act.astype(bf16).astype(f32)
        with_heavy = found[3:4]
        with_light = found[4:5] - with_heavy
        hsum[0:HID, :] += fold(act * with_light)
        hsum[HID:, :] += fold(act * with_heavy)
        return carry

    lax.fori_loop(0, STEPS, geometry, 0)

    msg0 = (mm(pair_out_t, hsum[...].astype(bf16)) * scale).astype(bf16)
    upd0 = mm(w_upd0_t, msg0)
    gate0 = sigmoid(upd0)
    act0 = upd0 * gate0
    slope0 = gate0 + act0 * (1.0 - gate0)
    layer_one = (jnp.where(heavy > 0.5, heavy_col, light_col) + act0).astype(bf16)
    send_b[...] = mm_nt(face_hot, layer_one).astype(bf16)
    b_right = halo(2, send_b.at[pl.ds(0, FACES)], recv_b.at[pl.ds(0, FACES)], right)
    b_left = halo(3, send_b.at[pl.ds(FACES, FACES)], recv_b.at[pl.ds(FACES, FACES)], left)
    b_right.start()
    b_left.start()
    own_sources = mm(w_msg1_t, layer_one).astype(bf16)

    def second_radial(step, carry):
        cols = pl.ds(pl.multiple_of(step * LANES, LANES), LANES)
        pre = mm(w_in_t[HID:], basis_buf[:, cols])
        gate = sigmoid(pre)
        act = pre * gate
        d1_buf[:, cols] = (gate + act * (1.0 - gate)).astype(bf16)
        rad_buf[:, cols] = mm(w_out1_t, act.astype(bf16))
        return carry

    lax.fori_loop(0, STEPS, second_radial, 0)

    b_right.wait_recv()
    b_left.wait_recv()
    ghost_sources = mm_nt(w_msg1_t, recv_b[...]).astype(bf16)
    sources = jnp.concatenate([own_sources, ghost_sources], axis=1)
    msum[...] = jnp.zeros_like(msum)

    def gather(step, carry):
        cols = pl.ds(pl.multiple_of(step * LANES, LANES), LANES)
        found = mm(sources, hot[:, cols])
        gat_buf[:, cols] = found.astype(bf16)
        msum[...] += fold(found * rad_buf[:, cols])
        return carry

    lax.fori_loop(0, STEPS, gather, 0)

    msg1 = (msum[...] * scale).astype(bf16)
    upd1 = mm(w_upd1_t, msg1)
    gate1 = sigmoid(upd1)
    slope1 = gate1 + upd1 * gate1 * (1.0 - gate1)
    d_msg1 = mm(wupd_ref[1], (energy_col * slope1).astype(bf16)) * scale

    ghost_sum[...] = jnp.zeros_like(ghost_sum)

    def ghost_terms(step, carry):
        cols = pl.ds(pl.multiple_of(step * LANES, LANES), LANES)
        terms = (rad_buf[:, cols] * tile(d_msg1)).astype(bf16)
        dt_buf[:, cols] = terms
        ghost_sum[...] += mm_nt(hot[ATOMS:, cols], terms)
        return carry

    lax.fori_loop(0, STEPS, ghost_terms, 0)
    send_c[...] = ghost_sum[...].astype(bf16)
    c_left = halo(4, send_c.at[pl.ds(0, FACES)], recv_c.at[pl.ds(0, FACES)], left)
    c_right = halo(5, send_c.at[pl.ds(FACES, FACES)], recv_c.at[pl.ds(FACES, FACES)], right)
    c_left.start()
    c_right.start()

    msum[...] = jnp.zeros_like(msum)

    def own_terms(step, carry):
        cols = pl.ds(pl.multiple_of(step * LANES, LANES), LANES)
        msum[...] += mm_nt(dt_buf[:, cols], hot[:ATOMS, cols])
        d_rad = (gat_buf[:, cols].astype(f32) * tile(d_msg1)).astype(bf16)
        d_pre = (mm(w_out1, d_rad) * d1_buf[:, cols].astype(f32)).astype(bf16)
        d_basis = mm(w_in_b[:, HID:], d_pre)
        db_buf[:, cols] = d_basis[0:8] + d_basis[8:16]
        return carry

    lax.fori_loop(0, STEPS, own_terms, 0)
    d_one = mm(wmsg_ref[1], msum[...].astype(bf16)) + energy_col

    c_left.wait_recv()
    c_right.wait_recv()
    d_one += mm(mm_nt(wmsg_ref[1], recv_c[...]).astype(bf16), face_hot)
    d_msg0 = mm(wupd_ref[0], (d_one * slope0).astype(bf16)) * scale
    d_hid0 = mm(pair_out, d_msg0.astype(bf16))
    d_light, d_heavy = d_hid0[:HID], d_hid0[HID:]

    msum[0:8, :] = jnp.zeros((8, ATOMS), f32)
    fghost[...] = jnp.zeros_like(fghost)

    def first_back(step, carry):
        cols = pl.ds(pl.multiple_of(step * LANES, LANES), LANES)
        found = mask_buf[:, cols]
        with_heavy = found[3:4]
        with_light = found[4:5] - with_heavy
        d_act = tile(d_light) * with_light + tile(d_heavy) * with_heavy
        d_pre = (d_act * d0_buf[:, cols].astype(f32)).astype(bf16)
        d_basis = mm(w_in_b[:, :HID], d_pre)
        d_basis = d_basis[0:8] + d_basis[8:16] + db_buf[:, cols]
        d_dist = jnp.sum(d_basis * slope_buf[:, cols], axis=0, keepdims=True)
        pull = unit_buf[:, cols] * d_dist
        msum[0:8, :] += fold(pull)
        pull_hi = pull.astype(bf16).astype(f32)
        pulls = jnp.concatenate([pull_hi, pull - pull_hi], axis=0).astype(bf16)
        f_buf[:, cols] = pulls
        fghost[...] += mm_nt(pulls, hot[ATOMS:, cols])
        return carry

    lax.fori_loop(0, STEPS, first_back, 0)
    send_d[...] = fghost[0:8, :] + fghost[8:16, :]
    d_left = halo(6, send_d, recv_d.at[0], left)
    d_right = halo(7, send_d, recv_d.at[1], right)
    d_left.start()
    d_right.start()

    msum[16:32, :] = jnp.zeros((16, ATOMS), f32)

    def own_pulls(step, carry):
        cols = pl.ds(pl.multiple_of(step * LANES, LANES), LANES)
        msum[16:32, :] += mm_nt(f_buf[:, cols], hot[:ATOMS, cols])
        return carry

    lax.fori_loop(0, STEPS, own_pulls, 0)
    force8 = msum[0:8, :] - msum[16:24, :] - msum[24:32, :]

    d_left.wait_recv()
    d_right.wait_recv()
    returned = jnp.where(lane_g < FACES, recv_d[0], recv_d[1])
    force8 = force8 - join_rows(mm(split_rows(returned), face_hot))

    kick8 = (0.5 * time_step) * force8
    for c in range(3):
        force_ref[c] = force8[c : c + 1]
    pos8[...] = jnp.zeros_like(pos8)
    for c in range(3):
        pos8[c : c + 1, :] = mom_ref[c]
    p_all[0] = pos8[...] + kick8
    p_copies = [to_bead(1, p_all, gap) for gap in range(1, beads)]
    for copy in p_copies:
        copy.start()

    mass = jnp.where(heavy > 0.5, heavy_mass, light_mass)
    cosine, reach, pull = mode_mix(beads)
    for copy in q_copies:
        copy.wait_recv()
    new_q = jnp.zeros((8, ATOMS), f32)
    new_p = jnp.zeros((8, ATOMS), f32)
    for gap in range(beads):
        new_q += cosine[gap] * q_all[gap]
        new_p += (pull[gap] * mass) * q_all[gap]
    for copy in p_copies:
        copy.wait_recv()
    from_p = jnp.zeros((8, ATOMS), f32)
    for gap in range(beads):
        from_p += reach[gap] * p_all[gap]
        new_p += cosine[gap] * p_all[gap]
    new_q += from_p / mass
    for c in range(3):
        newq_ref[c] = new_q[c : c + 1]
        newp_ref[c] = new_p[c : c + 1]

    for copy in (a_right, a_left, b_right, b_left, c_left, c_right, d_left, d_right):
        copy.wait_send()
    for copy in q_copies + p_copies:
        copy.wait_send()


def per_device(
    positions,
    momenta,
    species,
    neighbours,
    send_low,
    send_high,
    species_embed,
    w_radial_in,
    w_radial_out,
    w_message,
    w_update,
    w_energy,
):
    beads = lax.axis_size("bead")
    slabs = lax.axis_size("space")
    vmem = pl.BlockSpec(memory_space=pltpu.VMEM)
    result = jax.ShapeDtypeStruct((3, 1, ATOMS), f32)
    outs = pl.pallas_call(
        functools.partial(kernel, beads, slabs),
        out_shape=(result, result, result),
        in_specs=[vmem] * 12,
        out_specs=(vmem, vmem, vmem),
        scratch_shapes=[
            pltpu.VMEM((8, ATOMS), f32),
            pltpu.VMEM((128, CH), f32),
            pltpu.VMEM((128, 2 * HID), f32),
            pltpu.VMEM((EXT, EDGES), bf16),
            pltpu.VMEM((32, EXT), bf16),
            pltpu.VMEM((32, EDGES), bf16),
            pltpu.VMEM((8, EDGES), f32),
            pltpu.VMEM((8, EDGES), f32),
            pltpu.VMEM((8, EDGES), f32),
            pltpu.VMEM((HID, EDGES), bf16),
            pltpu.VMEM((HID, EDGES), bf16),
            pltpu.VMEM((CH, EDGES), f32),
            pltpu.VMEM((CH, EDGES), bf16),
            pltpu.VMEM((CH, EDGES), bf16),
            pltpu.VMEM((8, EDGES), f32),
            pltpu.VMEM((16, EDGES), bf16),
            pltpu.VMEM((2 * HID, ATOMS), f32),
            pltpu.VMEM((CH, ATOMS), f32),
            pltpu.VMEM((2 * FACES, CH), f32),
            pltpu.VMEM((16, 2 * FACES), f32),
            pltpu.VMEM((8, 2 * FACES), f32),
            pltpu.VMEM((2, 8, 2 * FACES), f32),
            pltpu.VMEM((2 * FACES, CH), bf16),
            pltpu.VMEM((2 * FACES, CH), bf16),
            pltpu.VMEM((2 * FACES, CH), bf16),
            pltpu.VMEM((2 * FACES, CH), bf16),
            pltpu.VMEM((8, 2 * FACES), f32),
            pltpu.VMEM((2, 8, 2 * FACES), f32),
            pltpu.VMEM((beads, 8, ATOMS), f32),
            pltpu.VMEM((beads, 8, ATOMS), f32),
            pltpu.SemaphoreType.DMA((8,)),
            pltpu.SemaphoreType.DMA((8,)),
            pltpu.SemaphoreType.DMA((2 * beads,)),
            pltpu.SemaphoreType.DMA((2 * beads,)),
        ],
        compiler_params=pltpu.CompilerParams(
            collective_id=0, has_side_effects=True, vmem_limit_bytes=48 * 1024 * 1024
        ),
    )(
        jnp.transpose(positions, (1, 0, 2)),
        jnp.transpose(momenta, (1, 0, 2)),
        species.reshape(1, ATOMS),
        neighbours.T,
        send_low.reshape(1, FACES),
        send_high.reshape(1, FACES),
        species_embed,
        w_radial_in,
        w_radial_out,
        w_message,
        w_update,
        w_energy.reshape(1, CH),
    )
    return tuple(jnp.transpose(out, (1, 0, 2)) for out in outs)


def solution(mesh):
    in_specs = (
        P("bead", None, "space"),
        P("bead", None, "space"),
        P("space"),
        P("space", None),
        P("space"),
        P("space"),
        P(),
        P(),
        P(),
        P(),
        P(),
        P(),
    )
    out_specs = (P("bead", None, "space"), P("bead", None, "space"), P("bead", None, "space"))
    return jax.shard_map(
        per_device, mesh=mesh, in_specs=in_specs, out_specs=out_specs, check_vma=False
    )
```

```python
import functools

import jax
import jax.numpy as jnp
import numpy as np
from jax import lax
from jax.experimental import pallas as pl
from jax.experimental.pallas import tpu as pltpu
from jax.sharding import PartitionSpec as P

cutoff_radius = 8.0
slab_width = 3.0
soft_square = 0.25
time_step = 0.5
cycle_angle = 2.0
light_mass = 1.0
heavy_mass = 16.0

ATOMS = 256
FACES = 64
SLOTS = 24
CH = 128
HID = 64
GROUP = 4
LANES = GROUP * ATOMS
STEPS = SLOTS // GROUP
EDGES = SLOTS * ATOMS
EXT = ATOMS + 2 * FACES

f32 = jnp.float32
bf16 = jnp.bfloat16
NT = (((1,), (1,)), ((), ()))


def mm(a, b):
    return jnp.dot(a, b, preferred_element_type=f32)


def mm_nt(a, b):
    return lax.dot_general(a, b, NT, preferred_element_type=f32)


def split_rows(x):
    hi = x.astype(bf16).astype(f32)
    mid = (x - hi).astype(bf16).astype(f32)
    low = x - hi - mid
    return jnp.concatenate([hi, mid, low, jnp.zeros_like(x)], axis=0).astype(bf16)


def join_rows(y):
    return y[0:8] + y[8:16] + y[16:24]


def tile(a):
    return jnp.concatenate([a] * GROUP, axis=1)


def fold(a):
    total = a[:, :ATOMS]
    for u in range(1, GROUP):
        total = total + a[:, u * ATOMS : (u + 1) * ATOMS]
    return total


def sigmoid(x):
    return 0.5 * jnp.tanh(0.5 * x) + 0.5


def sin_pi(z, zz):
    acc = -np.pi**11 / 39916800.0
    for c in (np.pi**9 / 362880.0, -np.pi**7 / 5040.0, np.pi**5 / 120.0, -np.pi**3 / 6.0, np.pi):
        acc = acc * zz + float(c)
    return acc * z


def cos_pi(zz):
    acc = np.pi**12 / 479001600.0
    for c in (
        -np.pi**10 / 3628800.0,
        np.pi**8 / 40320.0,
        -np.pi**6 / 720.0,
        np.pi**4 / 24.0,
        -np.pi**2 / 2.0,
        1.0,
    ):
        acc = acc * zz + float(c)
    return acc


def mode_mix(bead_count):
    k = np.arange(bead_count)
    angle = 2.0 * cycle_angle * np.sin(np.pi * k / bead_count)
    sinc = np.where(k > 0, np.sin(angle) / np.where(k > 0, angle, 1.0), 1.0)
    weights = (np.cos(angle), time_step * sinc, -angle * np.sin(angle) / time_step)
    gap = np.cos(2.0 * np.pi * k[:, None] * k[None, :] / bead_count) / bead_count
    return [[float(v) for v in gap @ w] for w in weights]


def kernel(
    beads,
    slabs,
    pos_hbm,
    mom_hbm,
    spec_hbm,
    nbr_hbm,
    low_hbm,
    high_hbm,
    emb_hbm,
    win_hbm,
    wout_hbm,
    wmsg_hbm,
    wupd_hbm,
    wen_hbm,
    out_ref,
    pos_ref,
    mom_ref,
    spec_ref,
    nbr_ref,
    low_ref,
    high_ref,
    emb_ref,
    win_ref,
    wout_ref,
    wmsg_ref,
    wupd_ref,
    wen_ref,
    pos8,
    small8,
    win32,
    hot,
    ext32,
    basis_buf,
    slope_buf,
    unit_buf,
    mask_buf,
    d0_buf,
    d1_buf,
    rad_buf,
    gat_buf,
    dt_buf,
    db_buf,
    f_buf,
    hsum,
    msum,
    ghost_sum,
    fghost,
    send_a,
    recv_a,
    send_b,
    recv_b,
    send_c,
    recv_c,
    send_d,
    recv_d,
    q_all,
    p_all,
    halo_send,
    halo_recv,
    bead_send,
    bead_recv,
    load_sem,
):
    bead = lax.axis_index("bead")
    slab = lax.axis_index("space")
    left = lax.rem(slab + slabs - 1, slabs)
    right = lax.rem(slab + 1, slabs)

    def halo(n, src, dst, target):
        return pltpu.make_async_remote_copy(
            src_ref=src,
            dst_ref=dst,
            send_sem=halo_send.at[n],
            recv_sem=halo_recv.at[n],
            device_id=(bead, target),
            device_id_type=pl.DeviceIdType.MESH,
        )

    def to_bead(n, buf, gap):
        return pltpu.make_async_remote_copy(
            src_ref=buf.at[0],
            dst_ref=buf.at[beads - gap],
            send_sem=bead_send.at[n * beads + gap],
            recv_sem=bead_recv.at[n * beads + beads - gap],
            device_id=(lax.rem(bead + gap, beads), slab),
            device_id_type=pl.DeviceIdType.MESH,
        )

    sources_hbm = (
        pos_hbm,
        spec_hbm,
        low_hbm,
        high_hbm,
        nbr_hbm,
        emb_hbm,
        win_hbm,
        wout_hbm,
        wmsg_hbm,
        wupd_hbm,
        wen_hbm,
        mom_hbm,
    )
    targets = (
        pos_ref,
        spec_ref,
        low_ref,
        high_ref,
        nbr_ref,
        emb_ref,
        win_ref,
        wout_ref,
        wmsg_ref,
        wupd_ref,
        wen_ref,
        mom_ref,
    )
    loads = [
        pltpu.make_async_copy(src, dst, load_sem.at[n])
        for n, (src, dst) in enumerate(zip(sources_hbm, targets))
    ]
    for load in loads:
        load.start()

    barrier = pltpu.get_barrier_semaphore()
    for target in (left, right):
        pl.semaphore_signal(
            barrier, inc=1, device_id=(bead, target), device_id_type=pl.DeviceIdType.MESH
        )
    for gap in range(1, beads):
        pl.semaphore_signal(
            barrier,
            inc=1,
            device_id=(lax.rem(bead + gap, beads), slab),
            device_id_type=pl.DeviceIdType.MESH,
        )

    for load in loads[:4]:
        load.wait()

    heavy = (spec_ref[...] == 1).astype(f32)
    pos8[...] = jnp.zeros_like(pos8)
    for c in range(3):
        pos8[c : c + 1, :] = pos_ref[c]
    own8 = pos8[...]
    q_all[0] = own8
    row8 = lax.broadcasted_iota(jnp.int32, (8, ATOMS), 0)
    code8 = own8 + jnp.where(row8 == 3, heavy, 0.0) + jnp.where(row8 == 4, 1.0, 0.0)

    face_row = jnp.concatenate([high_ref[...], low_ref[...]], axis=1)
    face_t = jnp.where(
        lax.broadcasted_iota(jnp.int32, (ATOMS, 2 * FACES), 0) == face_row, 1.0, 0.0
    )
    face_hot_t = face_t.astype(bf16)
    face_hot = face_t.T.astype(bf16)
    own32 = split_rows(code8)
    send_a[...] = join_rows(mm(own32, face_hot_t))

    pl.semaphore_wait(barrier, beads + 1)
    a_right = halo(0, send_a, recv_a.at[0], right)
    a_left = halo(1, send_a, recv_a.at[1], left)
    a_right.start()
    a_left.start()
    q_copies = [to_bead(0, q_all, gap) for gap in range(1, beads)]
    for copy in q_copies:
        copy.start()

    for load in loads[4:]:
        load.wait()

    ext_iota = lax.broadcasted_iota(jnp.int32, (EXT, ATOMS), 0)

    def build(step, carry):
        for u in range(GROUP):
            slot = step * GROUP + u
            row = nbr_ref[pl.ds(slot, 1), :]
            hot[:, pl.ds(pl.multiple_of(slot * ATOMS, ATOMS), ATOMS)] = jnp.where(
                ext_iota == row, 1.0, 0.0
            ).astype(bf16)
        return carry

    lax.fori_loop(0, STEPS, build, 0)

    w8 = jnp.concatenate([win_ref[0], win_ref[1]], axis=1)
    w8_hi = w8.astype(bf16).astype(f32)
    w8_low = w8 - w8_hi
    win32[...] = jnp.zeros_like(win32)
    win32[0:8, :] = w8_hi
    win32[8:16, :] = w8_hi
    win32[16:24, :] = w8_low
    w_in_t = win32[...].T[:, :32].astype(bf16)
    w_in_b = jnp.concatenate([w8_hi, w8_low], axis=0).astype(bf16)
    small8[...] = jnp.zeros_like(small8)
    small8[0:2, :] = emb_ref[...]
    small8[2:3, :] = wen_ref[...]
    columns = small8[...].T
    light_col, heavy_col, energy_col = columns[:, 0:1], columns[:, 1:2], columns[:, 2:3]
    kinds = mm(small8[0:8, :].astype(bf16), wmsg_ref[0]).astype(bf16).astype(f32)
    w_out0 = wout_ref[0].astype(f32)
    pair_out = jnp.concatenate([w_out0 * kinds[0:1, :], w_out0 * kinds[1:2, :]], axis=0)
    pair_out_t = pair_out.T.astype(bf16)
    pair_out = pair_out.astype(bf16)
    w_out1 = wout_ref[1]
    w_out1_t = w_out1.astype(f32).T.astype(bf16)
    w_upd0_t = wupd_ref[0].astype(f32).T.astype(bf16)
    w_upd1_t = wupd_ref[1].astype(f32).T.astype(bf16)
    w_msg1_t = wmsg_ref[1].astype(f32).T.astype(bf16)
    scale = float(1.0 / np.sqrt(SLOTS))

    a_right.wait_recv()
    a_left.wait_recv()
    row_g = lax.broadcasted_iota(jnp.int32, (8, 2 * FACES), 0)
    lane_g = lax.broadcasted_iota(jnp.int32, (8, 2 * FACES), 1)
    shift = jnp.where(row_g == 2, jnp.where(lane_g < FACES, -slab_width, slab_width), 0.0)
    ghost8 = jnp.where(lane_g < FACES, recv_a[0], recv_a[1]) + shift
    ext32[:, :ATOMS] = own32
    ext32[:, ATOMS:] = split_rows(ghost8)

    orders = lax.broadcasted_iota(jnp.int32, (8, LANES), 0).astype(f32) + 1.0
    is_xyz = lax.broadcasted_iota(jnp.int32, (8, LANES), 0) < 3

    hsum[...] = jnp.zeros_like(hsum)

    def geometry(step, carry):
        cols = pl.ds(pl.multiple_of(step * LANES, LANES), LANES)
        found = join_rows(mm(ext32[...], hot[:, cols]))
        mask_buf[:, cols] = found
        away = jnp.where(is_xyz, found - tile(own8), 0.0)
        square = jnp.sum(away * away, axis=0, keepdims=True) + soft_square
        inverse = lax.rsqrt(square)
        scaled = square * inverse * (1.0 / cutoff_radius)
        unit_buf[:, cols] = away * inverse
        phase = orders * scaled
        whole = jnp.floor(phase + 0.5)
        z = phase - whole
        sign = 1.0 - 2.0 * (whole - 2.0 * jnp.floor(whole * 0.5))
        zz = z * z
        sine = sign * sin_pi(z, zz)
        cosine = sign * cos_pi(zz)
        rest = 1.0 - scaled * scaled
        ratio = rest * rest * inverse
        ratio_slope = -(0.5 * scaled * rest + ratio) * inverse
        waves = sine * ratio
        slope_buf[:, cols] = cosine * (orders * (ratio * (np.pi / cutoff_radius))) + (
            sine * ratio_slope
        )
        waves_hi = waves.astype(bf16).astype(f32)
        stack = jnp.concatenate(
            [waves_hi, waves - waves_hi, waves_hi, jnp.zeros_like(waves)], axis=0
        ).astype(bf16)
        basis_buf[:, cols] = stack
        pre = mm(w_in_t[:HID], stack)
        gate = sigmoid(pre)
        act = pre * gate
        d0_buf[:, cols] = (gate + act * (1.0 - gate)).astype(bf16)
        act = act.astype(bf16).astype(f32)
        with_heavy = found[3:4]
        with_light = found[4:5] - with_heavy
        hsum[0:HID, :] += fold(act * with_light)
        hsum[HID:, :] += fold(act * with_heavy)
        return carry

    lax.fori_loop(0, STEPS, geometry, 0)

    msg0 = (mm(pair_out_t, hsum[...].astype(bf16)) * scale).astype(bf16)
    upd0 = mm(w_upd0_t, msg0)
    gate0 = sigmoid(upd0)
    act0 = upd0 * gate0
    slope0 = gate0 + act0 * (1.0 - gate0)
    layer_one = (jnp.where(heavy > 0.5, heavy_col, light_col) + act0).astype(bf16)
    send_b[...] = mm_nt(face_hot, layer_one).astype(bf16)
    b_right = halo(2, send_b.at[pl.ds(0, FACES)], recv_b.at[pl.ds(0, FACES)], right)
    b_left = halo(3, send_b.at[pl.ds(FACES, FACES)], recv_b.at[pl.ds(FACES, FACES)], left)
    b_right.start()
    b_left.start()
    own_sources = mm(w_msg1_t, layer_one).astype(bf16)

    def second_radial(step, carry):
        cols = pl.ds(pl.multiple_of(step * LANES, LANES), LANES)
        pre = mm(w_in_t[HID:], basis_buf[:, cols])
        gate = sigmoid(pre)
        act = pre * gate
        d1_buf[:, cols] = (gate + act * (1.0 - gate)).astype(bf16)
        rad_buf[:, cols] = mm(w_out1_t, act.astype(bf16))
        return carry

    lax.fori_loop(0, STEPS, second_radial, 0)

    b_right.wait_recv()
    b_left.wait_recv()
    ghost_sources = mm_nt(w_msg1_t, recv_b[...]).astype(bf16)
    sources = jnp.concatenate([own_sources, ghost_sources], axis=1)
    msum[...] = jnp.zeros_like(msum)

    def gather(step, carry):
        cols = pl.ds(pl.multiple_of(step * LANES, LANES), LANES)
        found = mm(sources, hot[:, cols])
        gat_buf[:, cols] = found.astype(bf16)
        msum[...] += fold(found * rad_buf[:, cols])
        return carry

    lax.fori_loop(0, STEPS, gather, 0)

    msg1 = (msum[...] * scale).astype(bf16)
    upd1 = mm(w_upd1_t, msg1)
    gate1 = sigmoid(upd1)
    slope1 = gate1 + upd1 * gate1 * (1.0 - gate1)
    d_msg1 = mm(wupd_ref[1], (energy_col * slope1).astype(bf16)) * scale

    ghost_sum[...] = jnp.zeros_like(ghost_sum)

    def ghost_terms(step, carry):
        cols = pl.ds(pl.multiple_of(step * LANES, LANES), LANES)
        terms = (rad_buf[:, cols] * tile(d_msg1)).astype(bf16)
        dt_buf[:, cols] = terms
        ghost_sum[...] += mm_nt(hot[ATOMS:, cols], terms)
        return carry

    lax.fori_loop(0, STEPS, ghost_terms, 0)
    send_c[...] = ghost_sum[...].astype(bf16)
    c_left = halo(4, send_c.at[pl.ds(0, FACES)], recv_c.at[pl.ds(0, FACES)], left)
    c_right = halo(5, send_c.at[pl.ds(FACES, FACES)], recv_c.at[pl.ds(FACES, FACES)], right)
    c_left.start()
    c_right.start()

    msum[...] = jnp.zeros_like(msum)

    def own_terms(step, carry):
        cols = pl.ds(pl.multiple_of(step * LANES, LANES), LANES)
        msum[...] += mm_nt(dt_buf[:, cols], hot[:ATOMS, cols])
        d_rad = (gat_buf[:, cols].astype(f32) * tile(d_msg1)).astype(bf16)
        d_pre = (mm(w_out1, d_rad) * d1_buf[:, cols].astype(f32)).astype(bf16)
        d_basis = mm(w_in_b[:, HID:], d_pre)
        db_buf[:, cols] = d_basis[0:8] + d_basis[8:16]
        return carry

    lax.fori_loop(0, STEPS, own_terms, 0)
    d_one = mm(wmsg_ref[1], msum[...].astype(bf16)) + energy_col

    c_left.wait_recv()
    c_right.wait_recv()
    d_one += mm(mm_nt(wmsg_ref[1], recv_c[...]).astype(bf16), face_hot)
    d_msg0 = mm(wupd_ref[0], (d_one * slope0).astype(bf16)) * scale
    d_hid0 = mm(pair_out, d_msg0.astype(bf16))
    d_light, d_heavy = d_hid0[:HID], d_hid0[HID:]

    msum[0:8, :] = jnp.zeros((8, ATOMS), f32)
    fghost[...] = jnp.zeros_like(fghost)

    def first_back(step, carry):
        cols = pl.ds(pl.multiple_of(step * LANES, LANES), LANES)
        found = mask_buf[:, cols]
        with_heavy = found[3:4]
        with_light = found[4:5] - with_heavy
        d_act = tile(d_light) * with_light + tile(d_heavy) * with_heavy
        d_pre = (d_act * d0_buf[:, cols].astype(f32)).astype(bf16)
        d_basis = mm(w_in_b[:, :HID], d_pre)
        d_basis = d_basis[0:8] + d_basis[8:16] + db_buf[:, cols]
        d_dist = jnp.sum(d_basis * slope_buf[:, cols], axis=0, keepdims=True)
        pull = unit_buf[:, cols] * d_dist
        msum[0:8, :] += fold(pull)
        pull_hi = pull.astype(bf16).astype(f32)
        pulls = jnp.concatenate([pull_hi, pull - pull_hi], axis=0).astype(bf16)
        f_buf[:, cols] = pulls
        fghost[...] += mm_nt(pulls, hot[ATOMS:, cols])
        return carry

    lax.fori_loop(0, STEPS, first_back, 0)
    send_d[...] = fghost[0:8, :] + fghost[8:16, :]
    d_left = halo(6, send_d, recv_d.at[0], left)
    d_right = halo(7, send_d, recv_d.at[1], right)
    d_left.start()
    d_right.start()

    msum[16:32, :] = jnp.zeros((16, ATOMS), f32)

    def own_pulls(step, carry):
        cols = pl.ds(pl.multiple_of(step * LANES, LANES), LANES)
        msum[16:32, :] += mm_nt(f_buf[:, cols], hot[:ATOMS, cols])
        return carry

    lax.fori_loop(0, STEPS, own_pulls, 0)
    force8 = msum[0:8, :] - msum[16:24, :] - msum[24:32, :]

    d_left.wait_recv()
    d_right.wait_recv()
    returned = jnp.where(lane_g < FACES, recv_d[0], recv_d[1])
    force8 = force8 - join_rows(mm(split_rows(returned), face_hot))

    kick8 = (0.5 * time_step) * force8
    for c in range(3):
        out_ref[6 + c] = force8[c : c + 1]
    pos8[...] = jnp.zeros_like(pos8)
    for c in range(3):
        pos8[c : c + 1, :] = mom_ref[c]
    p_all[0] = pos8[...] + kick8
    p_copies = [to_bead(1, p_all, gap) for gap in range(1, beads)]
    for copy in p_copies:
        copy.start()

    mass = jnp.where(heavy > 0.5, heavy_mass, light_mass)
    cosine, reach, pull = mode_mix(beads)
    for copy in q_copies:
        copy.wait_recv()
    new_q = jnp.zeros((8, ATOMS), f32)
    new_p = jnp.zeros((8, ATOMS), f32)
    for gap in range(beads):
        new_q += cosine[gap] * q_all[gap]
        new_p += (pull[gap] * mass) * q_all[gap]
    for copy in p_copies:
        copy.wait_recv()
    from_p = jnp.zeros((8, ATOMS), f32)
    for gap in range(beads):
        from_p += reach[gap] * p_all[gap]
        new_p += cosine[gap] * p_all[gap]
    new_q += from_p / mass
    for c in range(3):
        out_ref[c] = new_q[c : c + 1]
        out_ref[3 + c] = new_p[c : c + 1]

    for copy in (a_right, a_left, b_right, b_left, c_left, c_right, d_left, d_right):
        copy.wait_send()
    for copy in q_copies + p_copies:
        copy.wait_send()


def per_device(
    positions,
    momenta,
    species,
    neighbours,
    send_low,
    send_high,
    species_embed,
    w_radial_in,
    w_radial_out,
    w_message,
    w_update,
    w_energy,
):
    beads = lax.axis_size("bead")
    slabs = lax.axis_size("space")
    vmem = pl.BlockSpec(memory_space=pltpu.VMEM)
    result = jax.ShapeDtypeStruct((9, 1, ATOMS), f32)
    piece = jax.ShapeDtypeStruct((3, 1, ATOMS), f32)
    moved = pl.pallas_call(
        functools.partial(kernel, beads, slabs),
        out_shape=result,
        in_specs=[pl.BlockSpec(memory_space=pltpu.HBM)] * 12,
        out_specs=vmem,
        scratch_shapes=[
            pltpu.VMEM((3, 1, ATOMS), f32),
            pltpu.VMEM((3, 1, ATOMS), f32),
            pltpu.VMEM((1, ATOMS), jnp.int32),
            pltpu.VMEM((SLOTS, ATOMS), jnp.int32),
            pltpu.VMEM((1, FACES), jnp.int32),
            pltpu.VMEM((1, FACES), jnp.int32),
            pltpu.VMEM((2, CH), f32),
            pltpu.VMEM((2, 8, HID), f32),
            pltpu.VMEM((2, HID, CH), bf16),
            pltpu.VMEM((2, CH, CH), bf16),
            pltpu.VMEM((2, CH, CH), bf16),
            pltpu.VMEM((1, CH), f32),
            pltpu.VMEM((8, ATOMS), f32),
            pltpu.VMEM((128, CH), f32),
            pltpu.VMEM((128, 2 * HID), f32),
            pltpu.VMEM((EXT, EDGES), bf16),
            pltpu.VMEM((32, EXT), bf16),
            pltpu.VMEM((32, EDGES), bf16),
            pltpu.VMEM((8, EDGES), f32),
            pltpu.VMEM((8, EDGES), f32),
            pltpu.VMEM((8, EDGES), f32),
            pltpu.VMEM((HID, EDGES), bf16),
            pltpu.VMEM((HID, EDGES), bf16),
            pltpu.VMEM((CH, EDGES), f32),
            pltpu.VMEM((CH, EDGES), bf16),
            pltpu.VMEM((CH, EDGES), bf16),
            pltpu.VMEM((8, EDGES), f32),
            pltpu.VMEM((16, EDGES), bf16),
            pltpu.VMEM((2 * HID, ATOMS), f32),
            pltpu.VMEM((CH, ATOMS), f32),
            pltpu.VMEM((2 * FACES, CH), f32),
            pltpu.VMEM((16, 2 * FACES), f32),
            pltpu.VMEM((8, 2 * FACES), f32),
            pltpu.VMEM((2, 8, 2 * FACES), f32),
            pltpu.VMEM((2 * FACES, CH), bf16),
            pltpu.VMEM((2 * FACES, CH), bf16),
            pltpu.VMEM((2 * FACES, CH), bf16),
            pltpu.VMEM((2 * FACES, CH), bf16),
            pltpu.VMEM((8, 2 * FACES), f32),
            pltpu.VMEM((2, 8, 2 * FACES), f32),
            pltpu.VMEM((beads, 8, ATOMS), f32),
            pltpu.VMEM((beads, 8, ATOMS), f32),
            pltpu.SemaphoreType.DMA((8,)),
            pltpu.SemaphoreType.DMA((8,)),
            pltpu.SemaphoreType.DMA((2 * beads,)),
            pltpu.SemaphoreType.DMA((2 * beads,)),
            pltpu.SemaphoreType.DMA((12,)),
        ],
        compiler_params=pltpu.CompilerParams(
            collective_id=0, has_side_effects=True, vmem_limit_bytes=60 * 1024 * 1024
        ),
    )(
        jnp.transpose(positions, (1, 0, 2)),
        jnp.transpose(momenta, (1, 0, 2)),
        species.reshape(1, ATOMS),
        neighbours.T,
        send_low.reshape(1, FACES),
        send_high.reshape(1, FACES),
        species_embed,
        w_radial_in,
        w_radial_out,
        w_message,
        w_update,
        w_energy.reshape(1, CH),
    )
    outs = [moved[3 * n : 3 * n + 3] for n in range(3)]
    return tuple(jnp.transpose(out, (1, 0, 2)) for out in outs)


def solution(mesh):
    in_specs = (
        P("bead", None, "space"),
        P("bead", None, "space"),
        P("space"),
        P("space", None),
        P("space"),
        P("space"),
        P(),
        P(),
        P(),
        P(),
        P(),
        P(),
    )
    out_specs = (P("bead", None, "space"), P("bead", None, "space"), P("bead", None, "space"))
    return jax.shard_map(
        per_device, mesh=mesh, in_specs=in_specs, out_specs=out_specs, check_vma=False
    )
```

```python
import functools

import jax
import jax.numpy as jnp
import numpy as np
from jax import lax
from jax.experimental import pallas as pl
from jax.experimental.pallas import tpu as pltpu
from jax.sharding import PartitionSpec as P

cutoff_radius = 8.0
slab_width = 3.0
soft_square = 0.25
time_step = 0.5
cycle_angle = 2.0
light_mass = 1.0
heavy_mass = 16.0

ATOMS = 256
FACES = 64
SLOTS = 24
CH = 128
HID = 64
GROUPS = {
    "build": 12,
    "geometry": 12,
    "second_radial": 12,
    "gather": 12,
    "ghost_terms": 12,
    "own_terms": 12,
    "first_back": 12,
    "own_pulls": 12,
}
EDGES = SLOTS * ATOMS
EXT = ATOMS + 2 * FACES

f32 = jnp.float32
bf16 = jnp.bfloat16
NT = (((1,), (1,)), ((), ()))


def mm(a, b):
    return jnp.dot(a, b, preferred_element_type=f32)


def mm_nt(a, b):
    return lax.dot_general(a, b, NT, preferred_element_type=f32)


def split_rows(x):
    hi = x.astype(bf16).astype(f32)
    mid = (x - hi).astype(bf16).astype(f32)
    low = x - hi - mid
    return jnp.concatenate([hi, mid, low, jnp.zeros_like(x)], axis=0).astype(bf16)


def join_rows(y):
    return y[0:8] + y[8:16] + y[16:24]


def tile(a, group):
    return jnp.concatenate([a] * group, axis=1)


def fold(a):
    parts = [a[:, u * ATOMS : (u + 1) * ATOMS] for u in range(a.shape[1] // ATOMS)]
    while len(parts) > 1:
        pairs = [x + y for x, y in zip(parts[::2], parts[1::2])]
        parts = pairs + parts[2 * len(pairs) :]
    return parts[0]


def silu_of_half(y):
    t = jnp.tanh(y)
    u = y * t
    return y + u, (1.0 + t) * (1.0 + (y - u))


def over_slots(body):
    group = GROUPS[body.__name__]
    lanes = group * ATOMS

    def one(step, carry):
        body(group, step * group, pl.ds(pl.multiple_of(step * lanes, lanes), lanes))
        return carry

    lax.fori_loop(0, SLOTS // group, one, 0)


def sin_pi(z, zz):
    acc = -np.pi**11 / 39916800.0
    for c in (np.pi**9 / 362880.0, -np.pi**7 / 5040.0, np.pi**5 / 120.0, -np.pi**3 / 6.0, np.pi):
        acc = acc * zz + float(c)
    return acc * z


def cos_pi(zz):
    acc = np.pi**12 / 479001600.0
    for c in (
        -np.pi**10 / 3628800.0,
        np.pi**8 / 40320.0,
        -np.pi**6 / 720.0,
        np.pi**4 / 24.0,
        -np.pi**2 / 2.0,
        1.0,
    ):
        acc = acc * zz + float(c)
    return acc


def mode_mix(bead_count):
    k = np.arange(bead_count)
    angle = 2.0 * cycle_angle * np.sin(np.pi * k / bead_count)
    sinc = np.where(k > 0, np.sin(angle) / np.where(k > 0, angle, 1.0), 1.0)
    weights = (np.cos(angle), time_step * sinc, -angle * np.sin(angle) / time_step)
    gap = np.cos(2.0 * np.pi * k[:, None] * k[None, :] / bead_count) / bead_count
    return [[float(v) for v in gap @ w] for w in weights]


def kernel(
    beads,
    slabs,
    pos_hbm,
    mom_hbm,
    spec_hbm,
    nbr_hbm,
    low_hbm,
    high_hbm,
    emb_hbm,
    win_hbm,
    wout_hbm,
    wmsg_hbm,
    wupd_hbm,
    wen_hbm,
    out_ref,
    pos_ref,
    mom_ref,
    spec_ref,
    nbr_ref,
    low_ref,
    high_ref,
    emb_ref,
    win_ref,
    wout_ref,
    wmsg_ref,
    wupd_ref,
    wen_ref,
    pos8,
    small8,
    win32,
    hot,
    ext32,
    basis_buf,
    slope_buf,
    unit_buf,
    mask_buf,
    d0_buf,
    d1_buf,
    rad_buf,
    gat_buf,
    dt_buf,
    db_buf,
    f_buf,
    hsum,
    msum,
    ghost_sum,
    fghost,
    send_a,
    recv_a,
    send_b,
    recv_b,
    send_c,
    recv_c,
    send_d,
    recv_d,
    q_all,
    p_all,
    halo_send,
    halo_recv,
    bead_send,
    bead_recv,
    load_sem,
):
    bead = lax.axis_index("bead")
    slab = lax.axis_index("space")
    left = lax.rem(slab + slabs - 1, slabs)
    right = lax.rem(slab + 1, slabs)

    def halo(n, src, dst, target):
        return pltpu.make_async_remote_copy(
            src_ref=src,
            dst_ref=dst,
            send_sem=halo_send.at[n],
            recv_sem=halo_recv.at[n],
            device_id=(bead, target),
            device_id_type=pl.DeviceIdType.MESH,
        )

    def to_bead(n, buf, gap):
        return pltpu.make_async_remote_copy(
            src_ref=buf.at[0],
            dst_ref=buf.at[beads - gap],
            send_sem=bead_send.at[n * beads + gap],
            recv_sem=bead_recv.at[n * beads + beads - gap],
            device_id=(lax.rem(bead + gap, beads), slab),
            device_id_type=pl.DeviceIdType.MESH,
        )

    sources_hbm = (
        pos_hbm,
        spec_hbm,
        low_hbm,
        high_hbm,
        nbr_hbm,
        emb_hbm,
        win_hbm,
        wout_hbm,
        wmsg_hbm,
        wupd_hbm,
        wen_hbm,
        mom_hbm,
    )
    targets = (
        pos_ref,
        spec_ref,
        low_ref,
        high_ref,
        nbr_ref,
        emb_ref,
        win_ref,
        wout_ref,
        wmsg_ref,
        wupd_ref,
        wen_ref,
        mom_ref,
    )
    loads = [
        pltpu.make_async_copy(src, dst, load_sem.at[n])
        for n, (src, dst) in enumerate(zip(sources_hbm, targets))
    ]
    for load in loads:
        load.start()

    barrier = pltpu.get_barrier_semaphore()
    for target in (left, right):
        pl.semaphore_signal(
            barrier, inc=1, device_id=(bead, target), device_id_type=pl.DeviceIdType.MESH
        )
    for gap in range(1, beads):
        pl.semaphore_signal(
            barrier,
            inc=1,
            device_id=(lax.rem(bead + gap, beads), slab),
            device_id_type=pl.DeviceIdType.MESH,
        )

    for load in loads[:4]:
        load.wait()

    heavy = (spec_ref[...] == 1).astype(f32)
    pos8[...] = jnp.zeros_like(pos8)
    for c in range(3):
        pos8[c : c + 1, :] = pos_ref[c]
    own8 = pos8[...]
    q_all[0] = own8[:, :CH] + pltpu.roll(own8[:, CH:], 4, 0)
    row8 = lax.broadcasted_iota(jnp.int32, (8, ATOMS), 0)
    code8 = own8 + jnp.where(row8 == 3, heavy, 0.0) + jnp.where(row8 == 4, 1.0, 0.0)

    face_row = jnp.concatenate([high_ref[...], low_ref[...]], axis=1)
    face_t = jnp.where(
        lax.broadcasted_iota(jnp.int32, (ATOMS, 2 * FACES), 0) == face_row, 1.0, 0.0
    )
    face_hot_t = face_t.astype(bf16)
    face_hot = face_t.T.astype(bf16)
    own32 = split_rows(code8)
    send_a[...] = join_rows(mm(own32, face_hot_t))

    pl.semaphore_wait(barrier, beads + 1)
    a_right = halo(0, send_a, recv_a.at[0], right)
    a_left = halo(1, send_a, recv_a.at[1], left)
    a_right.start()
    a_left.start()
    q_copies = [to_bead(0, q_all, gap) for gap in range(1, beads)]
    for copy in q_copies:
        copy.start()

    for load in loads[4:]:
        load.wait()

    ext_iota = lax.broadcasted_iota(jnp.int32, (EXT, ATOMS), 0)

    def build(group, first, cols):
        for u in range(group):
            slot = first + u
            row = nbr_ref[pl.ds(slot, 1), :]
            hot[:, pl.ds(pl.multiple_of(slot * ATOMS, ATOMS), ATOMS)] = jnp.where(
                ext_iota == row, 1.0, 0.0
            ).astype(bf16)

    over_slots(build)

    w8 = jnp.concatenate([win_ref[0], win_ref[1]], axis=1)
    w8_hi = w8.astype(bf16).astype(f32)
    w8_low = w8 - w8_hi
    win32[...] = jnp.zeros_like(win32)
    win32[0:8, :] = w8_hi
    win32[8:16, :] = w8_hi
    win32[16:24, :] = w8_low
    w_in_t = (0.5 * win32[...].T[:, :32]).astype(bf16)
    w_in_b = (0.5 * jnp.concatenate([w8_hi, w8_low], axis=0)).astype(bf16)
    small8[...] = jnp.zeros_like(small8)
    small8[0:2, :] = emb_ref[...]
    small8[2:3, :] = wen_ref[...]
    columns = small8[...].T
    light_col, heavy_col, energy_col = columns[:, 0:1], columns[:, 1:2], columns[:, 2:3]
    kinds = mm(small8[0:8, :].astype(bf16), wmsg_ref[0]).astype(bf16).astype(f32)
    w_out0 = wout_ref[0].astype(f32)
    pair_out = jnp.concatenate([w_out0 * kinds[0:1, :], w_out0 * kinds[1:2, :]], axis=0)
    pair_out_t = pair_out.T.astype(bf16)
    pair_out = pair_out.astype(bf16)
    w_out1 = wout_ref[1]
    w_out1_t = w_out1.astype(f32).T.astype(bf16)
    w_upd0_t = wupd_ref[0].astype(f32).T.astype(bf16)
    w_upd1_t = wupd_ref[1].astype(f32).T.astype(bf16)
    w_msg1_t = wmsg_ref[1].astype(f32).T.astype(bf16)
    scale = float(1.0 / np.sqrt(SLOTS))
    front = (mm(w_upd0_t, pair_out_t) * (0.5 * scale)).astype(bf16)
    back = (mm(pair_out, wupd_ref[0]) * (0.25 * scale)).astype(bf16)
    is_heavy = jnp.where(
        lax.broadcasted_iota(jnp.int32, (8, CH), 0) < 4, heavy[:, :CH], heavy[:, CH:]
    )
    mass = jnp.where(is_heavy > 0.5, heavy_mass, light_mass)
    inverse_mass = jnp.where(is_heavy > 0.5, 1.0 / heavy_mass, 1.0 / light_mass)
    pos8[...] = jnp.zeros_like(pos8)
    for c in range(3):
        pos8[c : c + 1, :] = mom_ref[c]
    mom8 = pos8[...]

    a_right.wait_recv()
    a_left.wait_recv()
    row_g = lax.broadcasted_iota(jnp.int32, (8, 2 * FACES), 0)
    lane_g = lax.broadcasted_iota(jnp.int32, (8, 2 * FACES), 1)
    shift = jnp.where(row_g == 2, jnp.where(lane_g < FACES, -slab_width, slab_width), 0.0)
    ghost8 = jnp.where(lane_g < FACES, recv_a[0], recv_a[1]) + shift
    ext32[:, :ATOMS] = own32
    ext32[:, ATOMS:] = split_rows(ghost8)

    hsum[...] = jnp.zeros_like(hsum)

    def geometry(group, first, cols):
        rows = lax.broadcasted_iota(jnp.int32, (8, group * ATOMS), 0)
        orders = rows.astype(f32) + 1.0
        is_xyz = rows < 3
        found = join_rows(mm(ext32[...], hot[:, cols]))
        away = jnp.where(is_xyz, found - tile(own8, group), 0.0)
        square = jnp.sum(away * away, axis=0, keepdims=True) + soft_square
        inverse = lax.rsqrt(square)
        scaled = square * inverse * (1.0 / cutoff_radius)
        unit_buf[:, cols] = away * inverse
        phase = orders * scaled
        whole = jnp.floor(phase + 0.5)
        z = phase - whole
        sign = 1.0 - 2.0 * (whole - 2.0 * jnp.floor(whole * 0.5))
        zz = z * z
        sine = sign * sin_pi(z, zz)
        cosine = sign * cos_pi(zz)
        rest = 1.0 - scaled * scaled
        ratio = rest * rest * inverse
        ratio_slope = -(0.5 * scaled * rest + ratio) * inverse
        waves = sine * ratio
        slope_buf[:, cols] = cosine * (orders * (ratio * (np.pi / cutoff_radius))) + (
            sine * ratio_slope
        )
        waves_hi = waves.astype(bf16).astype(f32)
        stack = jnp.concatenate(
            [waves_hi, waves - waves_hi, waves_hi, jnp.zeros_like(waves)], axis=0
        ).astype(bf16)
        basis_buf[:, cols] = stack
        act, slope = silu_of_half(mm(w_in_t[:HID], stack))
        d0_buf[:, cols] = slope.astype(bf16)
        with_heavy = found[3:4]
        with_light = found[4:5] - with_heavy
        mask_buf[0:1, cols] = with_light
        mask_buf[1:2, cols] = with_heavy
        hsum[0:HID, :] += fold(act * with_light)
        hsum[HID:, :] += fold(act * with_heavy)

    over_slots(geometry)

    act0, slope0 = silu_of_half(mm(front, hsum[...].astype(bf16)))
    layer_one = (jnp.where(heavy > 0.5, heavy_col, light_col) + act0).astype(bf16)
    send_b[...] = mm_nt(face_hot, layer_one).astype(bf16)
    b_right = halo(2, send_b.at[pl.ds(0, FACES)], recv_b.at[pl.ds(0, FACES)], right)
    b_left = halo(3, send_b.at[pl.ds(FACES, FACES)], recv_b.at[pl.ds(FACES, FACES)], left)
    b_right.start()
    b_left.start()
    own_sources = mm(w_msg1_t, layer_one).astype(bf16)

    def second_radial(group, first, cols):
        act, slope = silu_of_half(mm(w_in_t[HID:], basis_buf[:, cols]))
        d1_buf[:, cols] = slope.astype(bf16)
        rad_buf[:, cols] = mm(w_out1_t, act.astype(bf16)).astype(bf16)

    over_slots(second_radial)

    b_right.wait_recv()
    b_left.wait_recv()
    ghost_sources = mm_nt(w_msg1_t, recv_b[...]).astype(bf16)
    sources = jnp.concatenate([own_sources, ghost_sources], axis=1)
    msum[...] = jnp.zeros_like(msum)

    def gather(group, first, cols):
        found = mm(sources, hot[:, cols])
        gat_buf[:, cols] = found.astype(bf16)
        msum[...] += fold(found * rad_buf[:, cols].astype(f32))

    over_slots(gather)

    msg1 = (msum[...] * (0.5 * scale)).astype(bf16)
    _, slope1 = silu_of_half(mm(w_upd1_t, msg1))
    d_msg1 = (mm(wupd_ref[1], (energy_col * slope1).astype(bf16)) * (0.5 * scale)).astype(bf16)

    ghost_sum[...] = jnp.zeros_like(ghost_sum)

    def ghost_terms(group, first, cols):
        terms = rad_buf[:, cols] * tile(d_msg1, group)
        dt_buf[:, cols] = terms
        ghost_sum[...] += mm_nt(hot[ATOMS:, cols], terms)

    over_slots(ghost_terms)
    send_c[...] = ghost_sum[...].astype(bf16)
    c_left = halo(4, send_c.at[pl.ds(0, FACES)], recv_c.at[pl.ds(0, FACES)], left)
    c_right = halo(5, send_c.at[pl.ds(FACES, FACES)], recv_c.at[pl.ds(FACES, FACES)], right)
    c_left.start()
    c_right.start()

    msum[...] = jnp.zeros_like(msum)

    def own_terms(group, first, cols):
        msum[...] += mm_nt(dt_buf[:, cols], hot[:ATOMS, cols])
        d_rad = gat_buf[:, cols] * tile(d_msg1, group)
        d_pre = mm(w_out1, d_rad).astype(bf16) * d1_buf[:, cols]
        d_basis = mm(w_in_b[:, HID:], d_pre)
        db_buf[:, cols] = d_basis[0:8] + d_basis[8:16]

    over_slots(own_terms)
    d_one = mm(wmsg_ref[1], msum[...].astype(bf16)) + energy_col

    c_left.wait_recv()
    c_right.wait_recv()
    d_one += mm(mm_nt(wmsg_ref[1], recv_c[...]).astype(bf16), face_hot)
    d_hid0 = mm(back, (d_one * (2.0 * slope0)).astype(bf16)).astype(bf16)
    d_light, d_heavy = d_hid0[:HID], d_hid0[HID:]

    msum[0:8, :] = jnp.zeros((8, ATOMS), f32)
    fghost[...] = jnp.zeros_like(fghost)

    def first_back(group, first, cols):
        with_light = mask_buf[0:1, cols].astype(bf16)
        with_heavy = mask_buf[1:2, cols].astype(bf16)
        d_act = tile(d_light, group) * with_light + tile(d_heavy, group) * with_heavy
        d_pre = d_act * d0_buf[:, cols]
        d_basis = mm(w_in_b[:, :HID], d_pre)
        d_basis = d_basis[0:8] + d_basis[8:16] + db_buf[:, cols]
        d_dist = jnp.sum(d_basis * slope_buf[:, cols], axis=0, keepdims=True)
        pull = unit_buf[:, cols] * d_dist
        msum[0:8, :] += fold(pull)
        pull_hi = pull.astype(bf16).astype(f32)
        pulls = jnp.concatenate([pull_hi, pull - pull_hi], axis=0).astype(bf16)
        f_buf[:, cols] = pulls
        fghost[...] += mm_nt(pulls, hot[ATOMS:, cols])

    over_slots(first_back)
    send_d[...] = fghost[0:8, :] + fghost[8:16, :]
    d_left = halo(6, send_d, recv_d.at[0], left)
    d_right = halo(7, send_d, recv_d.at[1], right)
    d_left.start()
    d_right.start()

    msum[16:32, :] = jnp.zeros((16, ATOMS), f32)

    def own_pulls(group, first, cols):
        msum[16:32, :] += mm_nt(f_buf[:, cols], hot[:ATOMS, cols])

    over_slots(own_pulls)
    force8 = msum[0:8, :] - msum[16:24, :] - msum[24:32, :]

    d_left.wait_recv()
    d_right.wait_recv()
    returned = jnp.where(lane_g < FACES, recv_d[0], recv_d[1])
    force8 = force8 - join_rows(mm(split_rows(returned), face_hot))

    kick8 = mom8 + (0.5 * time_step) * force8
    p_all[0] = kick8[:, :CH] + pltpu.roll(kick8[:, CH:], 4, 0)
    p_copies = [to_bead(1, p_all, gap) for gap in range(1, beads)]
    for copy in p_copies:
        copy.start()
    for c in range(3):
        out_ref[6 + c] = force8[c : c + 1]

    cosine, reach, pull = mode_mix(beads)
    for copy in q_copies:
        copy.wait_recv()
    new_q = jnp.zeros((8, CH), f32)
    new_p = jnp.zeros((8, CH), f32)
    for gap in range(beads):
        new_q += cosine[gap] * q_all[gap]
        new_p += pull[gap] * q_all[gap]
    new_p = new_p * mass
    for copy in p_copies:
        copy.wait_recv()
    from_p = jnp.zeros((8, CH), f32)
    for gap in range(beads):
        from_p += reach[gap] * p_all[gap]
        new_p += cosine[gap] * p_all[gap]
    new_q += from_p * inverse_mass
    for c in range(3):
        for half in range(2):
            row = c + 4 * half
            out_ref[c, :, half * CH : half * CH + CH] = new_q[row : row + 1]
            out_ref[3 + c, :, half * CH : half * CH + CH] = new_p[row : row + 1]

    for copy in (a_right, a_left, b_right, b_left, c_left, c_right, d_left, d_right):
        copy.wait_send()
    for copy in q_copies + p_copies:
        copy.wait_send()


def per_device(
    positions,
    momenta,
    species,
    neighbours,
    send_low,
    send_high,
    species_embed,
    w_radial_in,
    w_radial_out,
    w_message,
    w_update,
    w_energy,
):
    beads = lax.axis_size("bead")
    slabs = lax.axis_size("space")
    vmem = pl.BlockSpec(memory_space=pltpu.VMEM)
    result = jax.ShapeDtypeStruct((9, 1, ATOMS), f32)
    piece = jax.ShapeDtypeStruct((3, 1, ATOMS), f32)
    moved = pl.pallas_call(
        functools.partial(kernel, beads, slabs),
        out_shape=result,
        in_specs=[pl.BlockSpec(memory_space=pltpu.HBM)] * 12,
        out_specs=vmem,
        scratch_shapes=[
            pltpu.VMEM((3, 1, ATOMS), f32),
            pltpu.VMEM((3, 1, ATOMS), f32),
            pltpu.VMEM((1, ATOMS), jnp.int32),
            pltpu.VMEM((SLOTS, ATOMS), jnp.int32),
            pltpu.VMEM((1, FACES), jnp.int32),
            pltpu.VMEM((1, FACES), jnp.int32),
            pltpu.VMEM((2, CH), f32),
            pltpu.VMEM((2, 8, HID), f32),
            pltpu.VMEM((2, HID, CH), bf16),
            pltpu.VMEM((2, CH, CH), bf16),
            pltpu.VMEM((2, CH, CH), bf16),
            pltpu.VMEM((1, CH), f32),
            pltpu.VMEM((8, ATOMS), f32),
            pltpu.VMEM((128, CH), f32),
            pltpu.VMEM((128, 2 * HID), f32),
            pltpu.VMEM((EXT, EDGES), bf16),
            pltpu.VMEM((32, EXT), bf16),
            pltpu.VMEM((32, EDGES), bf16),
            pltpu.VMEM((8, EDGES), f32),
            pltpu.VMEM((8, EDGES), f32),
            pltpu.VMEM((8, EDGES), f32),
            pltpu.VMEM((HID, EDGES), bf16),
            pltpu.VMEM((HID, EDGES), bf16),
            pltpu.VMEM((CH, EDGES), bf16),
            pltpu.VMEM((CH, EDGES), bf16),
            pltpu.VMEM((CH, EDGES), bf16),
            pltpu.VMEM((8, EDGES), f32),
            pltpu.VMEM((16, EDGES), bf16),
            pltpu.VMEM((2 * HID, ATOMS), f32),
            pltpu.VMEM((CH, ATOMS), f32),
            pltpu.VMEM((2 * FACES, CH), f32),
            pltpu.VMEM((16, 2 * FACES), f32),
            pltpu.VMEM((8, 2 * FACES), f32),
            pltpu.VMEM((2, 8, 2 * FACES), f32),
            pltpu.VMEM((2 * FACES, CH), bf16),
            pltpu.VMEM((2 * FACES, CH), bf16),
            pltpu.VMEM((2 * FACES, CH), bf16),
            pltpu.VMEM((2 * FACES, CH), bf16),
            pltpu.VMEM((8, 2 * FACES), f32),
            pltpu.VMEM((2, 8, 2 * FACES), f32),
            pltpu.VMEM((beads, 8, CH), f32),
            pltpu.VMEM((beads, 8, CH), f32),
            pltpu.SemaphoreType.DMA((8,)),
            pltpu.SemaphoreType.DMA((8,)),
            pltpu.SemaphoreType.DMA((2 * beads,)),
            pltpu.SemaphoreType.DMA((2 * beads,)),
            pltpu.SemaphoreType.DMA((12,)),
        ],
        compiler_params=pltpu.CompilerParams(
            collective_id=0, has_side_effects=True, vmem_limit_bytes=60 * 1024 * 1024
        ),
    )(
        jnp.transpose(positions, (1, 0, 2)),
        jnp.transpose(momenta, (1, 0, 2)),
        species.reshape(1, ATOMS),
        neighbours.T,
        send_low.reshape(1, FACES),
        send_high.reshape(1, FACES),
        species_embed,
        w_radial_in,
        w_radial_out,
        w_message,
        w_update,
        w_energy.reshape(1, CH),
    )
    outs = [moved[3 * n : 3 * n + 3] for n in range(3)]
    return tuple(jnp.transpose(out, (1, 0, 2)) for out in outs)


def solution(mesh):
    in_specs = (
        P("bead", None, "space"),
        P("bead", None, "space"),
        P("space"),
        P("space", None),
        P("space"),
        P("space"),
        P(),
        P(),
        P(),
        P(),
        P(),
        P(),
    )
    out_specs = (P("bead", None, "space"), P("bead", None, "space"), P("bead", None, "space"))
    return jax.shard_map(
        per_device, mesh=mesh, in_specs=in_specs, out_specs=out_specs, check_vma=False
    )
```

```python
import functools

import jax
import jax.numpy as jnp
import numpy as np
from jax import lax
from jax.experimental import pallas as pl
from jax.experimental.pallas import tpu as pltpu
from jax.sharding import PartitionSpec as P

cutoff_radius = 8.0
slab_width = 3.0
soft_square = 0.25
time_step = 0.5
cycle_angle = 2.0
light_mass = 1.0
heavy_mass = 16.0

ATOMS = 256
FACES = 64
SLOTS = 24
CH = 128
HID = 64
GROUPS = {
    "build": 8,
    "geometry": 24,
    "second_radial": 24,
    "gather": 24,
    "ghost_terms": 24,
    "own_terms": 24,
    "first_back": 24,
    "own_pulls": 8,
}
EDGES = SLOTS * ATOMS
EXT = ATOMS + 2 * FACES

f32 = jnp.float32
bf16 = jnp.bfloat16
NT = (((1,), (1,)), ((), ()))


def mm(a, b):
    return jnp.dot(a, b, preferred_element_type=f32)


def mm_nt(a, b):
    return lax.dot_general(a, b, NT, preferred_element_type=f32)


def split_rows(x):
    hi = x.astype(bf16).astype(f32)
    mid = (x - hi).astype(bf16).astype(f32)
    low = x - hi - mid
    return jnp.concatenate([hi, mid, low, jnp.zeros_like(x)], axis=0).astype(bf16)


def join_rows(y):
    return y[0:8] + y[8:16] + y[16:24]


def tile(a, group):
    return jnp.concatenate([a] * group, axis=1)


def fold(a):
    parts = [a[:, u * ATOMS : (u + 1) * ATOMS] for u in range(a.shape[1] // ATOMS)]
    while len(parts) > 1:
        pairs = [x + y for x, y in zip(parts[::2], parts[1::2])]
        parts = pairs + parts[2 * len(pairs) :]
    return parts[0]


def silu_of_half(y):
    t = jnp.tanh(y)
    u = y * t
    return y + u, (1.0 + t) * (1.0 + (y - u))


def over_slots(body, once):
    group = GROUPS[body.__name__]
    lanes = group * ATOMS

    def one(step, carry):
        body(group, step * group, pl.ds(pl.multiple_of(step * lanes, lanes), lanes))
        return carry

    lax.fori_loop(0, once if group == SLOTS else SLOTS // group, one, 0)


def sin_pi(z, zz):
    acc = -np.pi**11 / 39916800.0
    for c in (np.pi**9 / 362880.0, -np.pi**7 / 5040.0, np.pi**5 / 120.0, -np.pi**3 / 6.0, np.pi):
        acc = acc * zz + float(c)
    return acc * z


def turn(phase):
    whole = jnp.floor(phase + 0.5)
    return 1.0 - 2.0 * (whole - 2.0 * jnp.floor(whole * 0.5)), phase - whole


def cos_pi(zz):
    acc = np.pi**12 / 479001600.0
    for c in (
        -np.pi**10 / 3628800.0,
        np.pi**8 / 40320.0,
        -np.pi**6 / 720.0,
        np.pi**4 / 24.0,
        -np.pi**2 / 2.0,
        1.0,
    ):
        acc = acc * zz + float(c)
    return acc


def mode_mix(bead_count):
    k = np.arange(bead_count)
    angle = 2.0 * cycle_angle * np.sin(np.pi * k / bead_count)
    sinc = np.where(k > 0, np.sin(angle) / np.where(k > 0, angle, 1.0), 1.0)
    weights = (np.cos(angle), time_step * sinc, -angle * np.sin(angle) / time_step)
    gap = np.cos(2.0 * np.pi * k[:, None] * k[None, :] / bead_count) / bead_count
    return [[float(v) for v in gap @ w] for w in weights]


def kernel(
    beads,
    slabs,
    pos_hbm,
    mom_hbm,
    spec_hbm,
    nbr_hbm,
    low_hbm,
    high_hbm,
    emb_hbm,
    win_hbm,
    wout_hbm,
    wmsg_hbm,
    wupd_hbm,
    wen_hbm,
    out_ref,
    pos_ref,
    mom_ref,
    spec_ref,
    nbr_ref,
    low_ref,
    high_ref,
    emb_ref,
    win_ref,
    wout_ref,
    wmsg_ref,
    wupd_ref,
    wen_ref,
    pos8,
    small8,
    win32,
    hot,
    ext32,
    basis_buf,
    slope_buf,
    unit_buf,
    reach_buf,
    mask_buf,
    held_one,
    w_out1_buf,
    w_upd1_buf,
    w_msg1_buf,
    pair_buf,
    back_buf,
    source_buf,
    d0_buf,
    d1_buf,
    rad_buf,
    gat_buf,
    dt_buf,
    db_buf,
    f_buf,
    hsum,
    msum,
    ghost_sum,
    fghost,
    send_a,
    recv_a,
    send_b,
    recv_b,
    send_c,
    recv_c,
    send_d,
    recv_d,
    q_all,
    p_all,
    halo_send,
    halo_recv,
    bead_send,
    bead_recv,
    load_sem,
):
    bead = lax.axis_index("bead")
    slab = lax.axis_index("space")
    left = lax.rem(slab + slabs - 1, slabs)
    right = lax.rem(slab + 1, slabs)
    once = lax.div(slab + slabs, slabs)

    def halo(n, src, dst, target):
        return pltpu.make_async_remote_copy(
            src_ref=src,
            dst_ref=dst,
            send_sem=halo_send.at[n],
            recv_sem=halo_recv.at[n],
            device_id=(bead, target),
            device_id_type=pl.DeviceIdType.MESH,
        )

    def to_bead(n, buf, gap):
        return pltpu.make_async_remote_copy(
            src_ref=buf.at[0],
            dst_ref=buf.at[beads - gap],
            send_sem=bead_send.at[n * beads + gap],
            recv_sem=bead_recv.at[n * beads + beads - gap],
            device_id=(lax.rem(bead + gap, beads), slab),
            device_id_type=pl.DeviceIdType.MESH,
        )

    sources_hbm = (
        pos_hbm,
        spec_hbm,
        low_hbm,
        high_hbm,
        nbr_hbm,
        emb_hbm,
        win_hbm,
        wout_hbm,
        wmsg_hbm,
        wupd_hbm,
        wen_hbm,
        mom_hbm,
    )
    targets = (
        pos_ref,
        spec_ref,
        low_ref,
        high_ref,
        nbr_ref,
        emb_ref,
        win_ref,
        wout_ref,
        wmsg_ref,
        wupd_ref,
        wen_ref,
        mom_ref,
    )
    loads = [
        pltpu.make_async_copy(src, dst, load_sem.at[n])
        for n, (src, dst) in enumerate(zip(sources_hbm, targets))
    ]
    for load in loads[:4]:
        load.start()

    barrier = pltpu.get_barrier_semaphore()
    for target in (left, right):
        pl.semaphore_signal(
            barrier, inc=1, device_id=(bead, target), device_id_type=pl.DeviceIdType.MESH
        )
    for gap in range(1, beads):
        pl.semaphore_signal(
            barrier,
            inc=1,
            device_id=(lax.rem(bead + gap, beads), slab),
            device_id_type=pl.DeviceIdType.MESH,
        )

    for load in loads[4:]:
        load.start()
    for load in loads[:4]:
        load.wait()

    heavy = (spec_ref[...] == 1).astype(f32)
    pos8[...] = jnp.zeros_like(pos8)
    for c in range(3):
        pos8[c : c + 1, :] = pos_ref[c]
    own8 = pos8[...]
    q_all[0] = own8[:, :CH] + pltpu.roll(own8[:, CH:], 4, 0)
    row8 = lax.broadcasted_iota(jnp.int32, (8, ATOMS), 0)
    code8 = own8 + jnp.where(row8 == 3, heavy, 0.0) + jnp.where(row8 == 4, 1.0, 0.0)

    face_row = jnp.concatenate([high_ref[...], low_ref[...]], axis=1)
    face_t = jnp.where(
        lax.broadcasted_iota(jnp.int32, (ATOMS, 2 * FACES), 0) == face_row, 1.0, 0.0
    )
    face_hot_t = face_t.astype(bf16)
    face_hot = face_t.T.astype(bf16)
    own32 = split_rows(code8)
    send_a[...] = join_rows(mm(own32, face_hot_t))

    pl.semaphore_wait(barrier, beads + 1)
    a_right = halo(0, send_a, recv_a.at[0], right)
    a_left = halo(1, send_a, recv_a.at[1], left)
    a_right.start()
    a_left.start()

    for load in loads[4:]:
        load.wait()

    ext_iota = lax.broadcasted_iota(jnp.int32, (EXT, ATOMS), 0)

    def build(group, first, cols):
        for u in range(group):
            slot = first + u
            row = nbr_ref[pl.ds(slot, 1), :]
            hot[:, pl.ds(pl.multiple_of(slot * ATOMS, ATOMS), ATOMS)] = jnp.where(
                ext_iota == row, 1.0, 0.0
            ).astype(bf16)

    over_slots(build, once)

    w8 = jnp.concatenate([win_ref[0], win_ref[1]], axis=1)
    w8_hi = w8.astype(bf16).astype(f32)
    w8_low = w8 - w8_hi
    win32[...] = jnp.zeros_like(win32)
    win32[0:8, :] = w8_hi
    win32[8:16, :] = w8_hi
    win32[16:24, :] = w8_low
    w_in_t = (0.5 * win32[...].T[:, :32]).astype(bf16)
    w_in_b = (0.5 * jnp.concatenate([w8_hi, w8_low], axis=0)).astype(bf16)
    small8[...] = jnp.zeros_like(small8)
    small8[0:2, :] = emb_ref[...]
    small8[2:3, :] = wen_ref[...]
    columns = small8[...].T
    light_col, heavy_col, energy_col = columns[:, 0:1], columns[:, 1:2], columns[:, 2:3]
    kinds = mm(small8[0:8, :].astype(bf16), wmsg_ref[0]).astype(bf16).astype(f32)
    w_out0 = wout_ref[0].astype(f32)
    pair_out = jnp.concatenate([w_out0 * kinds[0:1, :], w_out0 * kinds[1:2, :]], axis=0)
    pair_out_t = pair_out.T.astype(bf16)
    pair_buf[...] = pair_out.astype(bf16)
    w_upd0_t = wupd_ref[0].astype(f32).T.astype(bf16)
    scale = float(1.0 / np.sqrt(SLOTS))
    front = (mm(w_upd0_t, pair_out_t) * (0.5 * scale)).astype(bf16)

    a_right.wait_recv()
    a_left.wait_recv()
    row_g = lax.broadcasted_iota(jnp.int32, (8, 2 * FACES), 0)
    lane_g = lax.broadcasted_iota(jnp.int32, (8, 2 * FACES), 1)
    shift = jnp.where(row_g == 2, jnp.where(lane_g < FACES, -slab_width, slab_width), 0.0)
    ghost8 = jnp.where(lane_g < FACES, recv_a[0], recv_a[1]) + shift
    ext32[:, :ATOMS] = own32
    ext32[:, ATOMS:] = split_rows(ghost8)

    hsum[...] = jnp.zeros_like(hsum)

    def geometry(group, first, cols):
        rows = lax.broadcasted_iota(jnp.int32, (8, group * ATOMS), 0)
        orders = rows.astype(f32) + 1.0
        is_xyz = rows < 3
        found = join_rows(mm(ext32[...], hot[:, cols]))
        away = jnp.where(is_xyz, found - tile(own8, group), 0.0)
        square = jnp.sum(away * away, axis=0, keepdims=True) + soft_square
        inverse = lax.rsqrt(square)
        scaled = square * inverse * (1.0 / cutoff_radius)
        unit_buf[:, cols] = away * inverse
        phase = orders * scaled
        sign, z = turn(phase)
        rest = 1.0 - scaled * scaled
        ratio = rest * rest * inverse
        waves = sign * sin_pi(z, z * z) * ratio
        reach_buf[0:1, cols] = scaled
        reach_buf[1:2, cols] = inverse
        waves_hi = waves.astype(bf16).astype(f32)
        stack = jnp.concatenate(
            [waves_hi, waves - waves_hi, waves_hi, jnp.zeros_like(waves)], axis=0
        ).astype(bf16)
        basis_buf[:, cols] = stack
        act, slope = silu_of_half(mm(w_in_t[:HID], stack))
        d0_buf[:, cols] = slope.astype(bf16)
        with_heavy = found[3:4]
        with_light = found[4:5] - with_heavy
        mask_buf[0:1, cols] = with_light
        mask_buf[1:2, cols] = with_heavy
        hsum[0:HID, :] += fold(act * with_light)
        hsum[HID:, :] += fold(act * with_heavy)

    over_slots(geometry, once)

    act0, slope0 = silu_of_half(mm(front, hsum[...].astype(bf16)))
    layer_one = (jnp.where(heavy > 0.5, heavy_col, light_col) + act0).astype(bf16)
    send_b[...] = mm_nt(face_hot, layer_one).astype(bf16)
    b_right = halo(2, send_b.at[pl.ds(0, FACES)], recv_b.at[pl.ds(0, FACES)], right)
    b_left = halo(3, send_b.at[pl.ds(FACES, FACES)], recv_b.at[pl.ds(FACES, FACES)], left)
    b_right.start()
    b_left.start()
    q_copies = [to_bead(0, q_all, gap) for gap in range(1, beads)]
    for copy in q_copies:
        copy.start()
    w_out1 = wout_ref[1]
    held_one[...] = layer_one

    def late_weights(step, carry):
        w_out1_buf[...] = wout_ref[1].astype(f32).T.astype(bf16)
        w_upd1_buf[...] = wupd_ref[1].astype(f32).T.astype(bf16)
        w_msg1_t = wmsg_ref[1].astype(f32).T.astype(bf16)
        w_msg1_buf[...] = w_msg1_t
        source_buf[:, :ATOMS] = mm(w_msg1_t, held_one[...]).astype(bf16)
        back_buf[...] = (mm(pair_buf[...], wupd_ref[0]) * (0.25 * scale)).astype(bf16)
        return carry

    lax.fori_loop(0, once, late_weights, 0)
    is_heavy = jnp.where(
        lax.broadcasted_iota(jnp.int32, (8, CH), 0) < 4, heavy[:, :CH], heavy[:, CH:]
    )
    mass = jnp.where(is_heavy > 0.5, heavy_mass, light_mass)
    inverse_mass = jnp.where(is_heavy > 0.5, 1.0 / heavy_mass, 1.0 / light_mass)
    pos8[...] = jnp.zeros_like(pos8)
    for c in range(3):
        pos8[c : c + 1, :] = mom_ref[c]
    mom8 = pos8[...]

    def second_radial(group, first, cols):
        rows = lax.broadcasted_iota(jnp.int32, (8, group * ATOMS), 0)
        orders = rows.astype(f32) + 1.0
        scaled = reach_buf[0:1, cols]
        inverse = reach_buf[1:2, cols]
        sign, z = turn(orders * scaled)
        zz = z * z
        rest = 1.0 - scaled * scaled
        ratio = rest * rest * inverse
        ratio_slope = -(0.5 * scaled * rest + ratio) * inverse
        slope_buf[:, cols] = sign * (
            cos_pi(zz) * (orders * (ratio * (np.pi / cutoff_radius))) + sin_pi(z, zz) * ratio_slope
        )
        act, slope = silu_of_half(mm(w_in_t[HID:], basis_buf[:, cols]))
        d1_buf[:, cols] = slope.astype(bf16)
        rad_buf[:, cols] = mm(w_out1_buf[...], act.astype(bf16)).astype(bf16)

    over_slots(second_radial, once)

    b_right.wait_recv()
    b_left.wait_recv()
    source_buf[:, ATOMS:] = mm_nt(w_msg1_buf[...], recv_b[...]).astype(bf16)
    msum[...] = jnp.zeros_like(msum)

    def gather(group, first, cols):
        found = mm(source_buf[...], hot[:, cols])
        gat_buf[:, cols] = found.astype(bf16)
        msum[...] += fold(found * rad_buf[:, cols].astype(f32))

    over_slots(gather, once)

    msg1 = (msum[...] * (0.5 * scale)).astype(bf16)
    _, slope1 = silu_of_half(mm(w_upd1_buf[...], msg1))
    d_msg1 = (mm(wupd_ref[1], (energy_col * slope1).astype(bf16)) * (0.5 * scale)).astype(bf16)

    ghost_sum[...] = jnp.zeros_like(ghost_sum)

    def ghost_terms(group, first, cols):
        terms = rad_buf[:, cols] * tile(d_msg1, group)
        dt_buf[:, cols] = terms
        ghost_sum[...] += mm_nt(hot[ATOMS:, cols], terms)

    over_slots(ghost_terms, once)
    send_c[...] = ghost_sum[...].astype(bf16)
    c_left = halo(4, send_c.at[pl.ds(0, FACES)], recv_c.at[pl.ds(0, FACES)], left)
    c_right = halo(5, send_c.at[pl.ds(FACES, FACES)], recv_c.at[pl.ds(FACES, FACES)], right)
    c_left.start()
    c_right.start()

    msum[...] = jnp.zeros_like(msum)

    def own_terms(group, first, cols):
        msum[...] += mm_nt(dt_buf[:, cols], hot[:ATOMS, cols])
        d_rad = gat_buf[:, cols] * tile(d_msg1, group)
        d_pre = mm(w_out1, d_rad).astype(bf16) * d1_buf[:, cols]
        d_basis = mm(w_in_b[:, HID:], d_pre)
        db_buf[:, cols] = d_basis[0:8] + d_basis[8:16]

    over_slots(own_terms, once)
    d_one = mm(wmsg_ref[1], msum[...].astype(bf16)) + energy_col

    c_left.wait_recv()
    c_right.wait_recv()
    d_one += mm(mm_nt(wmsg_ref[1], recv_c[...]).astype(bf16), face_hot)
    d_hid0 = mm(back_buf[...], (d_one * (2.0 * slope0)).astype(bf16)).astype(bf16)
    d_light, d_heavy = d_hid0[:HID], d_hid0[HID:]

    msum[0:8, :] = jnp.zeros((8, ATOMS), f32)
    fghost[...] = jnp.zeros_like(fghost)

    def first_back(group, first, cols):
        with_light = mask_buf[0:1, cols].astype(bf16)
        with_heavy = mask_buf[1:2, cols].astype(bf16)
        d_act = tile(d_light, group) * with_light + tile(d_heavy, group) * with_heavy
        d_pre = d_act * d0_buf[:, cols]
        d_basis = mm(w_in_b[:, :HID], d_pre)
        d_basis = d_basis[0:8] + d_basis[8:16] + db_buf[:, cols]
        d_dist = jnp.sum(d_basis * slope_buf[:, cols], axis=0, keepdims=True)
        pull = unit_buf[:, cols] * d_dist
        msum[0:8, :] += fold(pull)
        pull_hi = pull.astype(bf16).astype(f32)
        pulls = jnp.concatenate([pull_hi, pull - pull_hi], axis=0).astype(bf16)
        f_buf[:, cols] = pulls
        fghost[...] += mm_nt(pulls, hot[ATOMS:, cols])

    over_slots(first_back, once)
    send_d[...] = fghost[0:8, :] + fghost[8:16, :]
    d_left = halo(6, send_d, recv_d.at[0], left)
    d_right = halo(7, send_d, recv_d.at[1], right)
    d_left.start()
    d_right.start()

    msum[16:32, :] = jnp.zeros((16, ATOMS), f32)

    def own_pulls(group, first, cols):
        msum[16:32, :] += mm_nt(f_buf[:, cols], hot[:ATOMS, cols])

    over_slots(own_pulls, once)
    force8 = msum[0:8, :] - msum[16:24, :] - msum[24:32, :]

    d_left.wait_recv()
    d_right.wait_recv()
    returned = jnp.where(lane_g < FACES, recv_d[0], recv_d[1])
    force8 = force8 - join_rows(mm(split_rows(returned), face_hot))

    kick8 = mom8 + (0.5 * time_step) * force8
    p_all[0] = kick8[:, :CH] + pltpu.roll(kick8[:, CH:], 4, 0)
    p_copies = [to_bead(1, p_all, gap) for gap in range(1, beads)]
    for copy in p_copies:
        copy.start()
    for c in range(3):
        out_ref[6 + c] = force8[c : c + 1]

    cosine, reach, pull = mode_mix(beads)
    for copy in q_copies:
        copy.wait_recv()
    new_q = jnp.zeros((8, CH), f32)
    new_p = jnp.zeros((8, CH), f32)
    for gap in range(beads):
        new_q += cosine[gap] * q_all[gap]
        new_p += pull[gap] * q_all[gap]
    new_p = new_p * mass
    for copy in p_copies:
        copy.wait_recv()
    from_p = jnp.zeros((8, CH), f32)
    for gap in range(beads):
        from_p += reach[gap] * p_all[gap]
        new_p += cosine[gap] * p_all[gap]
    new_q += from_p * inverse_mass
    for c in range(3):
        for half in range(2):
            row = c + 4 * half
            out_ref[c, :, half * CH : half * CH + CH] = new_q[row : row + 1]
            out_ref[3 + c, :, half * CH : half * CH + CH] = new_p[row : row + 1]

    for copy in (a_right, a_left, b_right, b_left, c_left, c_right, d_left, d_right):
        copy.wait_send()
    for copy in q_copies + p_copies:
        copy.wait_send()


def per_device(
    positions,
    momenta,
    species,
    neighbours,
    send_low,
    send_high,
    species_embed,
    w_radial_in,
    w_radial_out,
    w_message,
    w_update,
    w_energy,
):
    beads = lax.axis_size("bead")
    slabs = lax.axis_size("space")
    vmem = pl.BlockSpec(memory_space=pltpu.VMEM)
    result = jax.ShapeDtypeStruct((9, 1, ATOMS), f32)
    piece = jax.ShapeDtypeStruct((3, 1, ATOMS), f32)
    moved = pl.pallas_call(
        functools.partial(kernel, beads, slabs),
        out_shape=result,
        in_specs=[pl.BlockSpec(memory_space=pltpu.HBM)] * 12,
        out_specs=vmem,
        scratch_shapes=[
            pltpu.VMEM((3, 1, ATOMS), f32),
            pltpu.VMEM((3, 1, ATOMS), f32),
            pltpu.VMEM((1, ATOMS), jnp.int32),
            pltpu.VMEM((SLOTS, ATOMS), jnp.int32),
            pltpu.VMEM((1, FACES), jnp.int32),
            pltpu.VMEM((1, FACES), jnp.int32),
            pltpu.VMEM((2, CH), f32),
            pltpu.VMEM((2, 8, HID), f32),
            pltpu.VMEM((2, HID, CH), bf16),
            pltpu.VMEM((2, CH, CH), bf16),
            pltpu.VMEM((2, CH, CH), bf16),
            pltpu.VMEM((1, CH), f32),
            pltpu.VMEM((8, ATOMS), f32),
            pltpu.VMEM((128, CH), f32),
            pltpu.VMEM((128, 2 * HID), f32),
            pltpu.VMEM((EXT, EDGES), bf16),
            pltpu.VMEM((32, EXT), bf16),
            pltpu.VMEM((32, EDGES), bf16),
            pltpu.VMEM((8, EDGES), f32),
            pltpu.VMEM((8, EDGES), f32),
            pltpu.VMEM((8, EDGES), f32),
            pltpu.VMEM((8, EDGES), f32),
            pltpu.VMEM((CH, ATOMS), bf16),
            pltpu.VMEM((CH, HID), bf16),
            pltpu.VMEM((CH, CH), bf16),
            pltpu.VMEM((CH, CH), bf16),
            pltpu.VMEM((CH, CH), bf16),
            pltpu.VMEM((CH, CH), bf16),
            pltpu.VMEM((CH, EXT), bf16),
            pltpu.VMEM((HID, EDGES), bf16),
            pltpu.VMEM((HID, EDGES), bf16),
            pltpu.VMEM((CH, EDGES), bf16),
            pltpu.VMEM((CH, EDGES), bf16),
            pltpu.VMEM((CH, EDGES), bf16),
            pltpu.VMEM((8, EDGES), f32),
            pltpu.VMEM((16, EDGES), bf16),
            pltpu.VMEM((2 * HID, ATOMS), f32),
            pltpu.VMEM((CH, ATOMS), f32),
            pltpu.VMEM((2 * FACES, CH), f32),
            pltpu.VMEM((16, 2 * FACES), f32),
            pltpu.VMEM((8, 2 * FACES), f32),
            pltpu.VMEM((2, 8, 2 * FACES), f32),
            pltpu.VMEM((2 * FACES, CH), bf16),
            pltpu.VMEM((2 * FACES, CH), bf16),
            pltpu.VMEM((2 * FACES, CH), bf16),
            pltpu.VMEM((2 * FACES, CH), bf16),
            pltpu.VMEM((8, 2 * FACES), f32),
            pltpu.VMEM((2, 8, 2 * FACES), f32),
            pltpu.VMEM((beads, 8, CH), f32),
            pltpu.VMEM((beads, 8, CH), f32),
            pltpu.SemaphoreType.DMA((8,)),
            pltpu.SemaphoreType.DMA((8,)),
            pltpu.SemaphoreType.DMA((2 * beads,)),
            pltpu.SemaphoreType.DMA((2 * beads,)),
            pltpu.SemaphoreType.DMA((12,)),
        ],
        compiler_params=pltpu.CompilerParams(
            collective_id=0, has_side_effects=True, vmem_limit_bytes=60 * 1024 * 1024
        ),
    )(
        jnp.transpose(positions, (1, 0, 2)),
        jnp.transpose(momenta, (1, 0, 2)),
        species.reshape(1, ATOMS),
        neighbours.T,
        send_low.reshape(1, FACES),
        send_high.reshape(1, FACES),
        species_embed,
        w_radial_in,
        w_radial_out,
        w_message,
        w_update,
        w_energy.reshape(1, CH),
    )
    outs = [moved[3 * n : 3 * n + 3] for n in range(3)]
    return tuple(jnp.transpose(out, (1, 0, 2)) for out in outs)


def solution(mesh):
    in_specs = (
        P("bead", None, "space"),
        P("bead", None, "space"),
        P("space"),
        P("space", None),
        P("space"),
        P("space"),
        P(),
        P(),
        P(),
        P(),
        P(),
        P(),
    )
    out_specs = (P("bead", None, "space"), P("bead", None, "space"), P("bead", None, "space"))
    return jax.shard_map(
        per_device, mesh=mesh, in_specs=in_specs, out_specs=out_specs, check_vma=False
    )
```

```python
import functools

import jax
import jax.numpy as jnp
import numpy as np
from jax import lax
from jax.experimental import pallas as pl
from jax.experimental.pallas import tpu as pltpu
from jax.sharding import PartitionSpec as P

cutoff_radius = 8.0
slab_width = 3.0
soft_square = 0.25
time_step = 0.5
cycle_angle = 2.0
light_mass = 1.0
heavy_mass = 16.0

ATOMS = 256
FACES = 64
SLOTS = 24
CH = 128
HID = 64
GROUPS = {
    "build": 8,
    "geometry": 24,
    "second_radial": 24,
    "gather": 24,
    "ghost_terms": 24,
    "own_terms": 24,
    "first_back": 24,
    "own_pulls": 8,
}
EDGES = SLOTS * ATOMS
EXT = ATOMS + 2 * FACES

f32 = jnp.float32
bf16 = jnp.bfloat16
NT = (((1,), (1,)), ((), ()))


def mm(a, b):
    return jnp.dot(a, b, preferred_element_type=f32)


def mm_nt(a, b):
    return lax.dot_general(a, b, NT, preferred_element_type=f32)


def split_rows(x):
    hi = x.astype(bf16).astype(f32)
    mid = (x - hi).astype(bf16).astype(f32)
    low = x - hi - mid
    return jnp.concatenate([hi, mid, low, jnp.zeros_like(x)], axis=0).astype(bf16)


def join_rows(y):
    return y[0:8] + y[8:16] + y[16:24]


def tile(a, group):
    return jnp.concatenate([a] * group, axis=1)


def fold(a):
    parts = [a[:, u * ATOMS : (u + 1) * ATOMS] for u in range(a.shape[1] // ATOMS)]
    while len(parts) > 1:
        pairs = [x + y for x, y in zip(parts[::2], parts[1::2])]
        parts = pairs + parts[2 * len(pairs) :]
    return parts[0]


def silu_of_half(y):
    t = jnp.tanh(y)
    u = y * t
    return y + u, (1.0 + t) * (1.0 + (y - u))


def over_slots(body, once):
    group = GROUPS[body.__name__]
    lanes = group * ATOMS

    def one(step, carry):
        body(group, step * group, pl.ds(pl.multiple_of(step * lanes, lanes), lanes))
        return carry

    lax.fori_loop(0, once if group == SLOTS else SLOTS // group, one, 0)


def sin_pi(z, zz):
    acc = -np.pi**11 / 39916800.0
    for c in (np.pi**9 / 362880.0, -np.pi**7 / 5040.0, np.pi**5 / 120.0, -np.pi**3 / 6.0, np.pi):
        acc = acc * zz + float(c)
    return acc * z


def turn(phase):
    whole = jnp.floor(phase + 0.5)
    return 1.0 - 2.0 * (whole - 2.0 * jnp.floor(whole * 0.5)), phase - whole


def cos_pi(zz):
    acc = np.pi**12 / 479001600.0
    for c in (
        -np.pi**10 / 3628800.0,
        np.pi**8 / 40320.0,
        -np.pi**6 / 720.0,
        np.pi**4 / 24.0,
        -np.pi**2 / 2.0,
        1.0,
    ):
        acc = acc * zz + float(c)
    return acc


def mode_mix(bead_count):
    k = np.arange(bead_count)
    angle = 2.0 * cycle_angle * np.sin(np.pi * k / bead_count)
    sinc = np.where(k > 0, np.sin(angle) / np.where(k > 0, angle, 1.0), 1.0)
    weights = (np.cos(angle), time_step * sinc, -angle * np.sin(angle) / time_step)
    gap = np.cos(2.0 * np.pi * k[:, None] * k[None, :] / bead_count) / bead_count
    return [[float(v) for v in gap @ w] for w in weights]


def kernel(
    beads,
    slabs,
    pos_hbm,
    mom_hbm,
    spec_hbm,
    nbr_hbm,
    low_hbm,
    high_hbm,
    emb_hbm,
    win_hbm,
    wout_hbm,
    wmsg_hbm,
    wupd_hbm,
    wen_hbm,
    out_ref,
    pos_ref,
    mom_ref,
    spec_ref,
    nbr_ref,
    low_ref,
    high_ref,
    emb_ref,
    win_ref,
    wout_ref,
    wmsg_ref,
    wupd_ref,
    wen_ref,
    pos8,
    small8,
    win32,
    hot,
    ext32,
    basis_buf,
    slope_buf,
    unit_buf,
    reach_buf,
    mask_buf,
    held_one,
    w_out1_buf,
    w_upd1_buf,
    w_msg1_buf,
    pair_buf,
    back_buf,
    source_buf,
    d0_buf,
    d1_buf,
    rad_buf,
    gat_buf,
    dt_buf,
    db_buf,
    f_buf,
    hsum,
    msum,
    ghost_sum,
    fghost,
    send_a,
    recv_a,
    send_b,
    recv_b,
    send_c,
    recv_c,
    send_d,
    recv_d,
    q_all,
    p_all,
    halo_send,
    halo_recv,
    bead_send,
    bead_recv,
    load_sem,
):
    bead = lax.axis_index("bead")
    slab = lax.axis_index("space")
    left = lax.rem(slab + slabs - 1, slabs)
    right = lax.rem(slab + 1, slabs)
    once = lax.div(slab + slabs, slabs)

    def halo(n, src, dst, target):
        return pltpu.make_async_remote_copy(
            src_ref=src,
            dst_ref=dst,
            send_sem=halo_send.at[n],
            recv_sem=halo_recv.at[n],
            device_id=(bead, target),
            device_id_type=pl.DeviceIdType.MESH,
        )

    def to_bead(n, buf, gap):
        return pltpu.make_async_remote_copy(
            src_ref=buf.at[0],
            dst_ref=buf.at[beads - gap],
            send_sem=bead_send.at[n * beads + gap],
            recv_sem=bead_recv.at[n * beads + beads - gap],
            device_id=(lax.rem(bead + gap, beads), slab),
            device_id_type=pl.DeviceIdType.MESH,
        )

    sources_hbm = (
        pos_hbm,
        spec_hbm,
        low_hbm,
        high_hbm,
        nbr_hbm,
        emb_hbm,
        win_hbm,
        wout_hbm,
        wmsg_hbm,
        wupd_hbm,
        wen_hbm,
        mom_hbm,
    )
    targets = (
        pos_ref,
        spec_ref,
        low_ref,
        high_ref,
        nbr_ref,
        emb_ref,
        win_ref,
        wout_ref,
        wmsg_ref,
        wupd_ref,
        wen_ref,
        mom_ref,
    )
    loads = [
        pltpu.make_async_copy(src, dst, load_sem.at[n])
        for n, (src, dst) in enumerate(zip(sources_hbm, targets))
    ]
    for load in loads[:4]:
        load.start()

    barrier = pltpu.get_barrier_semaphore()
    for target in (left, right):
        pl.semaphore_signal(
            barrier, inc=1, device_id=(bead, target), device_id_type=pl.DeviceIdType.MESH
        )
    for gap in range(1, beads):
        pl.semaphore_signal(
            barrier,
            inc=1,
            device_id=(lax.rem(bead + gap, beads), slab),
            device_id_type=pl.DeviceIdType.MESH,
        )

    for load in loads[4:]:
        load.start()
    for load in loads[:4]:
        load.wait()

    heavy = (spec_ref[...] == 1).astype(f32)
    pos8[...] = jnp.zeros_like(pos8)
    for c in range(3):
        pos8[c : c + 1, :] = pos_ref[c]
    own8 = pos8[...]
    q_all[0] = own8[:, :CH] + pltpu.roll(own8[:, CH:], 4, 0)
    row8 = lax.broadcasted_iota(jnp.int32, (8, ATOMS), 0)
    code8 = own8 + jnp.where(row8 == 3, heavy, 0.0) + jnp.where(row8 == 4, 1.0, 0.0)

    face_row = jnp.concatenate([high_ref[...], low_ref[...]], axis=1)
    face_t = jnp.where(
        lax.broadcasted_iota(jnp.int32, (ATOMS, 2 * FACES), 0) == face_row, 1.0, 0.0
    )
    face_hot_t = face_t.astype(bf16)
    face_hot = face_t.T.astype(bf16)
    own32 = split_rows(code8)
    send_a[...] = join_rows(mm(own32, face_hot_t))

    pl.semaphore_wait(barrier, beads + 1)
    a_right = halo(0, send_a, recv_a.at[0], right)
    a_left = halo(1, send_a, recv_a.at[1], left)
    a_right.start()
    a_left.start()

    for load in loads[4:]:
        load.wait()

    ext_iota = lax.broadcasted_iota(jnp.int32, (EXT, ATOMS), 0)

    def build(group, first, cols):
        for u in range(group):
            slot = first + u
            row = nbr_ref[pl.ds(slot, 1), :]
            hot[:, pl.ds(pl.multiple_of(slot * ATOMS, ATOMS), ATOMS)] = jnp.where(
                ext_iota == row, 1.0, 0.0
            ).astype(bf16)

    over_slots(build, once)

    w8 = jnp.concatenate([win_ref[0], win_ref[1]], axis=1)
    w8_hi = w8.astype(bf16).astype(f32)
    w8_low = w8 - w8_hi
    win32[...] = jnp.zeros_like(win32)
    win32[0:8, :] = w8_hi
    win32[8:16, :] = w8_hi
    win32[16:24, :] = w8_low
    w_in_t = (0.5 * win32[...].T[:, :32]).astype(bf16)
    w_in_b = (0.5 * jnp.concatenate([w8_hi, w8_low], axis=0)).astype(bf16)
    small8[...] = jnp.zeros_like(small8)
    small8[0:2, :] = emb_ref[...]
    small8[2:3, :] = wen_ref[...]
    columns = small8[...].T
    light_col, heavy_col, energy_col = columns[:, 0:1], columns[:, 1:2], columns[:, 2:3]
    kinds = mm(small8[0:8, :].astype(bf16), wmsg_ref[0]).astype(bf16).astype(f32)
    w_out0 = wout_ref[0].astype(f32)
    pair_out = jnp.concatenate([w_out0 * kinds[0:1, :], w_out0 * kinds[1:2, :]], axis=0)
    pair_out_t = pair_out.T.astype(bf16)
    pair_buf[...] = pair_out.astype(bf16)
    w_upd0_t = wupd_ref[0].astype(f32).T.astype(bf16)
    scale = float(1.0 / np.sqrt(SLOTS))
    front = (mm(w_upd0_t, pair_out_t) * (0.5 * scale)).astype(bf16)

    a_right.wait_recv()
    a_left.wait_recv()
    row_g = lax.broadcasted_iota(jnp.int32, (8, 2 * FACES), 0)
    lane_g = lax.broadcasted_iota(jnp.int32, (8, 2 * FACES), 1)
    shift = jnp.where(row_g == 2, jnp.where(lane_g < FACES, -slab_width, slab_width), 0.0)
    ghost8 = jnp.where(lane_g < FACES, recv_a[0], recv_a[1]) + shift
    ext32[:, :ATOMS] = own32
    ext32[:, ATOMS:] = split_rows(ghost8)

    hsum[...] = jnp.zeros_like(hsum)

    def geometry(group, first, cols):
        rows = lax.broadcasted_iota(jnp.int32, (8, group * ATOMS), 0)
        orders = rows.astype(f32) + 1.0
        is_xyz = rows < 3
        found = join_rows(mm(ext32[...], hot[:, cols]))
        away = jnp.where(is_xyz, found - tile(own8, group), 0.0)
        square = jnp.sum(away * away, axis=0, keepdims=True) + soft_square
        inverse = lax.rsqrt(square)
        scaled = square * inverse * (1.0 / cutoff_radius)
        unit_buf[:, cols] = away * inverse
        phase = orders * scaled
        sign, z = turn(phase)
        rest = 1.0 - scaled * scaled
        ratio = rest * rest * inverse
        waves = sign * sin_pi(z, z * z) * ratio
        reach_buf[0:1, cols] = scaled
        reach_buf[1:2, cols] = inverse
        waves_hi = waves.astype(bf16).astype(f32)
        stack = jnp.concatenate(
            [waves_hi, waves - waves_hi, waves_hi, jnp.zeros_like(waves)], axis=0
        ).astype(bf16)
        basis_buf[:, cols] = stack
        act, slope = silu_of_half(mm(w_in_t[:HID], stack))
        d0_buf[:, cols] = slope.astype(bf16)
        with_heavy = found[3:4]
        with_light = found[4:5] - with_heavy
        mask_buf[0:1, cols] = with_light
        mask_buf[1:2, cols] = with_heavy
        hsum[0:HID, :] += fold(act * with_light)
        hsum[HID:, :] += fold(act * with_heavy)

    over_slots(geometry, once)

    act0, slope0 = silu_of_half(mm(front, hsum[...].astype(bf16)))
    layer_one = (jnp.where(heavy > 0.5, heavy_col, light_col) + act0).astype(bf16)
    send_b[...] = mm_nt(face_hot, layer_one).astype(bf16)
    b_right = halo(2, send_b.at[pl.ds(0, FACES)], recv_b.at[pl.ds(0, FACES)], right)
    b_left = halo(3, send_b.at[pl.ds(FACES, FACES)], recv_b.at[pl.ds(FACES, FACES)], left)
    b_right.start()
    b_left.start()
    q_copies = [to_bead(0, q_all, gap) for gap in range(1, beads)]
    for copy in q_copies:
        copy.start()
    w_out1 = wout_ref[1]
    held_one[...] = layer_one

    def late_weights(step, carry):
        w_out1_buf[...] = wout_ref[1].astype(f32).T.astype(bf16)
        w_upd1_buf[...] = wupd_ref[1].astype(f32).T.astype(bf16)
        w_msg1_t = wmsg_ref[1].astype(f32).T.astype(bf16)
        w_msg1_buf[...] = w_msg1_t
        source_buf[:, :ATOMS] = mm(w_msg1_t, held_one[...]).astype(bf16)
        back_buf[...] = (mm(pair_buf[...], wupd_ref[0]) * (0.25 * scale)).astype(bf16)
        return carry

    lax.fori_loop(0, once, late_weights, 0)
    is_heavy = jnp.where(
        lax.broadcasted_iota(jnp.int32, (8, CH), 0) < 4, heavy[:, :CH], heavy[:, CH:]
    )
    mass = jnp.where(is_heavy > 0.5, heavy_mass, light_mass)
    inverse_mass = jnp.where(is_heavy > 0.5, 1.0 / heavy_mass, 1.0 / light_mass)
    pos8[...] = jnp.zeros_like(pos8)
    for c in range(3):
        pos8[c : c + 1, :] = mom_ref[c]
    mom8 = pos8[...]

    def second_radial(group, first, cols):
        rows = lax.broadcasted_iota(jnp.int32, (8, group * ATOMS), 0)
        orders = rows.astype(f32) + 1.0
        scaled = reach_buf[0:1, cols]
        inverse = reach_buf[1:2, cols]
        sign, z = turn(orders * scaled)
        zz = z * z
        rest = 1.0 - scaled * scaled
        ratio = rest * rest * inverse
        ratio_slope = -(0.5 * scaled * rest + ratio) * inverse
        slope_buf[:, cols] = sign * (
            cos_pi(zz) * (orders * (ratio * (np.pi / cutoff_radius))) + sin_pi(z, zz) * ratio_slope
        )
        act, slope = silu_of_half(mm(w_in_t[HID:], basis_buf[:, cols]))
        d1_buf[:, cols] = slope.astype(bf16)
        rad_buf[:, cols] = mm(w_out1_buf[...], act.astype(bf16)).astype(bf16)

    over_slots(second_radial, once)

    b_right.wait_recv()
    b_left.wait_recv()
    source_buf[:, ATOMS:] = mm_nt(w_msg1_buf[...], recv_b[...]).astype(bf16)
    msum[...] = jnp.zeros_like(msum)

    def gather(group, first, cols):
        found = mm(source_buf[...], hot[:, cols])
        gat_buf[:, cols] = found.astype(bf16)
        msum[...] += fold(found * rad_buf[:, cols].astype(f32))

    over_slots(gather, once)

    msg1 = (msum[...] * (0.5 * scale)).astype(bf16)
    _, slope1 = silu_of_half(mm(w_upd1_buf[...], msg1))
    d_msg1 = (mm(wupd_ref[1], (energy_col * slope1).astype(bf16)) * (0.5 * scale)).astype(bf16)

    ghost_sum[...] = jnp.zeros_like(ghost_sum)

    def ghost_terms(group, first, cols):
        terms = rad_buf[:, cols] * tile(d_msg1, group)
        dt_buf[:, cols] = terms
        ghost_sum[...] += mm_nt(hot[ATOMS:, cols], terms)

    over_slots(ghost_terms, once)
    send_c[...] = ghost_sum[...].astype(bf16)
    c_left = halo(4, send_c.at[pl.ds(0, FACES)], recv_c.at[pl.ds(0, FACES)], left)
    c_right = halo(5, send_c.at[pl.ds(FACES, FACES)], recv_c.at[pl.ds(FACES, FACES)], right)
    c_left.start()
    c_right.start()

    msum[...] = jnp.zeros_like(msum)

    def own_terms(group, first, cols):
        msum[...] += mm_nt(dt_buf[:, cols], hot[:ATOMS, cols])
        d_rad = gat_buf[:, cols] * tile(d_msg1, group)
        d_pre = mm(w_out1, d_rad).astype(bf16) * d1_buf[:, cols]
        d_basis = mm(w_in_b[:, HID:], d_pre)
        db_buf[:, cols] = d_basis[0:8] + d_basis[8:16]

    over_slots(own_terms, once)
    d_one = mm(wmsg_ref[1], msum[...].astype(bf16)) + energy_col

    c_left.wait_recv()
    c_right.wait_recv()
    d_one += mm(mm_nt(wmsg_ref[1], recv_c[...]).astype(bf16), face_hot)
    d_hid0 = mm(back_buf[...], (d_one * (2.0 * slope0)).astype(bf16)).astype(bf16)
    d_light, d_heavy = d_hid0[:HID], d_hid0[HID:]

    msum[0:8, :] = jnp.zeros((8, ATOMS), f32)
    fghost[...] = jnp.zeros_like(fghost)

    def first_back(group, first, cols):
        with_light = mask_buf[0:1, cols].astype(bf16)
        with_heavy = mask_buf[1:2, cols].astype(bf16)
        d_act = tile(d_light, group) * with_light + tile(d_heavy, group) * with_heavy
        d_pre = d_act * d0_buf[:, cols]
        d_basis = mm(w_in_b[:, :HID], d_pre)
        d_basis = d_basis[0:8] + d_basis[8:16] + db_buf[:, cols]
        d_dist = jnp.sum(d_basis * slope_buf[:, cols], axis=0, keepdims=True)
        pull = unit_buf[:, cols] * d_dist
        msum[0:8, :] += fold(pull)
        pull_hi = pull.astype(bf16).astype(f32)
        pulls = jnp.concatenate([pull_hi, pull - pull_hi], axis=0).astype(bf16)
        f_buf[:, cols] = pulls
        fghost[...] += mm_nt(pulls, hot[ATOMS:, cols])

    over_slots(first_back, once)
    send_d[...] = fghost[0:8, :] + fghost[8:16, :]
    d_left = halo(6, send_d, recv_d.at[0], left)
    d_right = halo(7, send_d, recv_d.at[1], right)
    d_left.start()
    d_right.start()

    msum[16:32, :] = jnp.zeros((16, ATOMS), f32)

    def own_pulls(group, first, cols):
        msum[16:32, :] += mm_nt(f_buf[:, cols], hot[:ATOMS, cols])

    over_slots(own_pulls, once)
    force8 = msum[0:8, :] - msum[16:24, :] - msum[24:32, :]

    d_left.wait_recv()
    d_right.wait_recv()
    returned = jnp.where(lane_g < FACES, recv_d[0], recv_d[1])
    force8 = force8 - join_rows(mm(split_rows(returned), face_hot))

    kick8 = mom8 + (0.5 * time_step) * force8
    p_all[0] = kick8[:, :CH] + pltpu.roll(kick8[:, CH:], 4, 0)
    p_copies = [to_bead(1, p_all, gap) for gap in range(1, beads)]
    for copy in p_copies:
        copy.start()
    for c in range(3):
        out_ref[6 + c] = force8[c : c + 1]

    cosine, reach, pull = mode_mix(beads)
    for copy in q_copies:
        copy.wait_recv()
    new_q = jnp.zeros((8, CH), f32)
    new_p = jnp.zeros((8, CH), f32)
    for gap in range(beads):
        new_q += cosine[gap] * q_all[gap]
        new_p += pull[gap] * q_all[gap]
    new_p = new_p * mass
    for copy in p_copies:
        copy.wait_recv()
    from_p = jnp.zeros((8, CH), f32)
    for gap in range(beads):
        from_p += reach[gap] * p_all[gap]
        new_p += cosine[gap] * p_all[gap]
    new_q += from_p * inverse_mass
    for c in range(3):
        for half in range(2):
            row = c + 4 * half
            out_ref[c, :, half * CH : half * CH + CH] = new_q[row : row + 1]
            out_ref[3 + c, :, half * CH : half * CH + CH] = new_p[row : row + 1]

    for copy in (a_right, a_left, b_right, b_left, c_left, c_right, d_left, d_right):
        copy.wait_send()
    for copy in q_copies + p_copies:
        copy.wait_send()


def per_device(
    positions,
    momenta,
    species,
    neighbours,
    send_low,
    send_high,
    species_embed,
    w_radial_in,
    w_radial_out,
    w_message,
    w_update,
    w_energy,
):
    beads = lax.axis_size("bead")
    slabs = lax.axis_size("space")
    vmem = pl.BlockSpec(memory_space=pltpu.VMEM)
    result = pltpu.VMEM((9, 1, ATOMS), f32)
    piece = jax.ShapeDtypeStruct((3, 1, ATOMS), f32)
    moved = pl.pallas_call(
        functools.partial(kernel, beads, slabs),
        out_shape=result,
        in_specs=[pl.BlockSpec(memory_space=pltpu.HBM)] * 12,
        out_specs=vmem,
        scratch_shapes=[
            pltpu.VMEM((3, 1, ATOMS), f32),
            pltpu.VMEM((3, 1, ATOMS), f32),
            pltpu.VMEM((1, ATOMS), jnp.int32),
            pltpu.VMEM((SLOTS, ATOMS), jnp.int32),
            pltpu.VMEM((1, FACES), jnp.int32),
            pltpu.VMEM((1, FACES), jnp.int32),
            pltpu.VMEM((2, CH), f32),
            pltpu.VMEM((2, 8, HID), f32),
            pltpu.VMEM((2, HID, CH), bf16),
            pltpu.VMEM((2, CH, CH), bf16),
            pltpu.VMEM((2, CH, CH), bf16),
            pltpu.VMEM((1, CH), f32),
            pltpu.VMEM((8, ATOMS), f32),
            pltpu.VMEM((128, CH), f32),
            pltpu.VMEM((128, 2 * HID), f32),
            pltpu.VMEM((EXT, EDGES), bf16),
            pltpu.VMEM((32, EXT), bf16),
            pltpu.VMEM((32, EDGES), bf16),
            pltpu.VMEM((8, EDGES), f32),
            pltpu.VMEM((8, EDGES), f32),
            pltpu.VMEM((8, EDGES), f32),
            pltpu.VMEM((8, EDGES), f32),
            pltpu.VMEM((CH, ATOMS), bf16),
            pltpu.VMEM((CH, HID), bf16),
            pltpu.VMEM((CH, CH), bf16),
            pltpu.VMEM((CH, CH), bf16),
            pltpu.VMEM((CH, CH), bf16),
            pltpu.VMEM((CH, CH), bf16),
            pltpu.VMEM((CH, EXT), bf16),
            pltpu.VMEM((HID, EDGES), bf16),
            pltpu.VMEM((HID, EDGES), bf16),
            pltpu.VMEM((CH, EDGES), bf16),
            pltpu.VMEM((CH, EDGES), bf16),
            pltpu.VMEM((CH, EDGES), bf16),
            pltpu.VMEM((8, EDGES), f32),
            pltpu.VMEM((16, EDGES), bf16),
            pltpu.VMEM((2 * HID, ATOMS), f32),
            pltpu.VMEM((CH, ATOMS), f32),
            pltpu.VMEM((2 * FACES, CH), f32),
            pltpu.VMEM((16, 2 * FACES), f32),
            pltpu.VMEM((8, 2 * FACES), f32),
            pltpu.VMEM((2, 8, 2 * FACES), f32),
            pltpu.VMEM((2 * FACES, CH), bf16),
            pltpu.VMEM((2 * FACES, CH), bf16),
            pltpu.VMEM((2 * FACES, CH), bf16),
            pltpu.VMEM((2 * FACES, CH), bf16),
            pltpu.VMEM((8, 2 * FACES), f32),
            pltpu.VMEM((2, 8, 2 * FACES), f32),
            pltpu.VMEM((beads, 8, CH), f32),
            pltpu.VMEM((beads, 8, CH), f32),
            pltpu.SemaphoreType.DMA((8,)),
            pltpu.SemaphoreType.DMA((8,)),
            pltpu.SemaphoreType.DMA((2 * beads,)),
            pltpu.SemaphoreType.DMA((2 * beads,)),
            pltpu.SemaphoreType.DMA((12,)),
        ],
        compiler_params=pltpu.CompilerParams(
            collective_id=0, has_side_effects=True, vmem_limit_bytes=60 * 1024 * 1024
        ),
    )(
        jnp.transpose(positions, (1, 0, 2)),
        jnp.transpose(momenta, (1, 0, 2)),
        species.reshape(1, ATOMS),
        neighbours.T,
        send_low.reshape(1, FACES),
        send_high.reshape(1, FACES),
        species_embed,
        w_radial_in,
        w_radial_out,
        w_message,
        w_update,
        w_energy.reshape(1, CH),
    )
    outs = [moved[3 * n : 3 * n + 3] for n in range(3)]
    return tuple(jnp.transpose(out, (1, 0, 2)) for out in outs)


def solution(mesh):
    in_specs = (
        P("bead", None, "space"),
        P("bead", None, "space"),
        P("space"),
        P("space", None),
        P("space"),
        P("space"),
        P(),
        P(),
        P(),
        P(),
        P(),
        P(),
    )
    out_specs = (P("bead", None, "space"), P("bead", None, "space"), P("bead", None, "space"))
    return jax.shard_map(
        per_device, mesh=mesh, in_specs=in_specs, out_specs=out_specs, check_vma=False
    )
```

```python
import functools

import jax
import jax.numpy as jnp
import numpy as np
from jax import lax
from jax.experimental import pallas as pl
from jax.experimental.pallas import tpu as pltpu
from jax.sharding import PartitionSpec as P

cutoff_radius = 8.0
slab_width = 3.0
soft_square = 0.25
time_step = 0.5
cycle_angle = 2.0
light_mass = 1.0
heavy_mass = 16.0

ATOMS = 256
FACES = 64
SLOTS = 24
CH = 128
HID = 64
GROUPS = {
    "build": 8,
    "geometry": 24,
    "second_radial": 24,
    "gather": 24,
    "ghost_terms": 24,
    "own_terms": 24,
    "first_back": 24,
    "own_pulls": 8,
}
EDGES = SLOTS * ATOMS
EXT = ATOMS + 2 * FACES

f32 = jnp.float32
bf16 = jnp.bfloat16
NT = (((1,), (1,)), ((), ()))


def mm(a, b):
    return jnp.dot(a, b, preferred_element_type=f32)


def mm_nt(a, b):
    return lax.dot_general(a, b, NT, preferred_element_type=f32)


def split_rows(x):
    hi = x.astype(bf16).astype(f32)
    mid = (x - hi).astype(bf16).astype(f32)
    low = x - hi - mid
    return jnp.concatenate([hi, mid, low, jnp.zeros_like(x)], axis=0).astype(bf16)


def join_rows(y):
    return y[0:8] + y[8:16] + y[16:24]


def tile(a, group):
    return jnp.concatenate([a] * group, axis=1)


def fold(a):
    parts = [a[:, u * ATOMS : (u + 1) * ATOMS] for u in range(a.shape[1] // ATOMS)]
    while len(parts) > 1:
        pairs = [x + y for x, y in zip(parts[::2], parts[1::2])]
        parts = pairs + parts[2 * len(pairs) :]
    return parts[0]


def silu_of_half(y):
    t = jnp.tanh(y)
    u = y * t
    return y + u, (1.0 + t) * (1.0 + (y - u))


def over_slots(body, once):
    group = GROUPS[body.__name__]
    lanes = group * ATOMS

    def one(step, carry):
        body(group, step * group, pl.ds(pl.multiple_of(step * lanes, lanes), lanes))
        return carry

    lax.fori_loop(0, once if group == SLOTS else SLOTS // group, one, 0)


def sin_pi(z, zz):
    acc = -np.pi**11 / 39916800.0
    for c in (np.pi**9 / 362880.0, -np.pi**7 / 5040.0, np.pi**5 / 120.0, -np.pi**3 / 6.0, np.pi):
        acc = acc * zz + float(c)
    return acc * z


def turn(phase):
    whole = jnp.floor(phase + 0.5)
    return 1.0 - 2.0 * (whole - 2.0 * jnp.floor(whole * 0.5)), phase - whole


def cos_pi(zz):
    acc = np.pi**12 / 479001600.0
    for c in (
        -np.pi**10 / 3628800.0,
        np.pi**8 / 40320.0,
        -np.pi**6 / 720.0,
        np.pi**4 / 24.0,
        -np.pi**2 / 2.0,
        1.0,
    ):
        acc = acc * zz + float(c)
    return acc


def mode_mix(bead_count):
    k = np.arange(bead_count)
    angle = 2.0 * cycle_angle * np.sin(np.pi * k / bead_count)
    sinc = np.where(k > 0, np.sin(angle) / np.where(k > 0, angle, 1.0), 1.0)
    weights = (np.cos(angle), time_step * sinc, -angle * np.sin(angle) / time_step)
    gap = np.cos(2.0 * np.pi * k[:, None] * k[None, :] / bead_count) / bead_count
    return [[float(v) for v in gap @ w] for w in weights]


def kernel(
    beads,
    slabs,
    pos_hbm,
    mom_hbm,
    spec_hbm,
    nbr_hbm,
    low_hbm,
    high_hbm,
    emb_hbm,
    win_hbm,
    wout_hbm,
    wmsg_hbm,
    wupd_hbm,
    wen_hbm,
    out_ref,
    pos_ref,
    mom_ref,
    spec_ref,
    nbr_ref,
    low_ref,
    high_ref,
    emb_ref,
    win_ref,
    wout_ref,
    wmsg_ref,
    wupd_ref,
    wen_ref,
    pos8,
    small8,
    win32,
    hot,
    ext32,
    basis_buf,
    slope_buf,
    unit_buf,
    reach_buf,
    mask_buf,
    held_one,
    w_out1_buf,
    w_upd1_buf,
    w_msg1_buf,
    pair_buf,
    back_buf,
    source_buf,
    d0_buf,
    d1_buf,
    rad_buf,
    gat_buf,
    dt_buf,
    db_buf,
    f_buf,
    hsum,
    msum,
    ghost_sum,
    fghost,
    send_a,
    recv_a,
    send_b,
    recv_b,
    send_c,
    recv_c,
    send_d,
    recv_d,
    q_all,
    p_all,
    halo_send,
    halo_recv,
    bead_send,
    bead_recv,
    load_sem,
):
    bead = lax.axis_index("bead")
    slab = lax.axis_index("space")
    left = lax.rem(slab + slabs - 1, slabs)
    right = lax.rem(slab + 1, slabs)
    once = lax.div(slab + slabs, slabs)

    def halo(n, src, dst, target):
        return pltpu.make_async_remote_copy(
            src_ref=src,
            dst_ref=dst,
            send_sem=halo_send.at[n],
            recv_sem=halo_recv.at[n],
            device_id=(bead, target),
            device_id_type=pl.DeviceIdType.MESH,
        )

    def to_bead(n, buf, gap):
        return pltpu.make_async_remote_copy(
            src_ref=buf.at[0],
            dst_ref=buf.at[beads - gap],
            send_sem=bead_send.at[n * beads + gap],
            recv_sem=bead_recv.at[n * beads + beads - gap],
            device_id=(lax.rem(bead + gap, beads), slab),
            device_id_type=pl.DeviceIdType.MESH,
        )

    sources_hbm = (
        pos_hbm,
        spec_hbm,
        low_hbm,
        high_hbm,
        nbr_hbm,
        emb_hbm,
        win_hbm,
        wout_hbm,
        wmsg_hbm,
        wupd_hbm,
        wen_hbm,
        mom_hbm,
    )
    targets = (
        pos_ref,
        spec_ref,
        low_ref,
        high_ref,
        nbr_ref,
        emb_ref,
        win_ref,
        wout_ref,
        wmsg_ref,
        wupd_ref,
        wen_ref,
        mom_ref,
    )
    loads = [
        pltpu.make_async_copy(src, dst, load_sem.at[n])
        for n, (src, dst) in enumerate(zip(sources_hbm, targets))
    ]
    barrier = pltpu.get_barrier_semaphore()
    for target in (left, right):
        pl.semaphore_signal(
            barrier, inc=1, device_id=(bead, target), device_id_type=pl.DeviceIdType.MESH
        )
    for load in loads[:4]:
        load.start()
    for gap in range(1, beads):
        pl.semaphore_signal(
            barrier,
            inc=1,
            device_id=(lax.rem(bead + gap, beads), slab),
            device_id_type=pl.DeviceIdType.MESH,
        )

    for load in loads[4:]:
        load.start()
    for load in loads[:4]:
        load.wait()

    heavy = (spec_ref[...] == 1).astype(f32)
    pos8[...] = jnp.zeros_like(pos8)
    for c in range(3):
        pos8[c : c + 1, :] = pos_ref[c]
    own8 = pos8[...]
    q_all[0] = own8[:, :CH] + pltpu.roll(own8[:, CH:], 4, 0)
    row8 = lax.broadcasted_iota(jnp.int32, (8, ATOMS), 0)
    code8 = own8 + jnp.where(row8 == 3, heavy, 0.0) + jnp.where(row8 == 4, 1.0, 0.0)

    face_row = jnp.concatenate([high_ref[...], low_ref[...]], axis=1)
    face_t = jnp.where(
        lax.broadcasted_iota(jnp.int32, (ATOMS, 2 * FACES), 0) == face_row, 1.0, 0.0
    )
    face_hot_t = face_t.astype(bf16)
    face_hot = face_t.T.astype(bf16)
    own32 = split_rows(code8)
    send_a[...] = join_rows(mm(own32, face_hot_t))

    pl.semaphore_wait(barrier, beads + 1)
    a_right = halo(0, send_a, recv_a.at[0], right)
    a_left = halo(1, send_a, recv_a.at[1], left)
    a_right.start()
    a_left.start()

    for load in loads[4:]:
        load.wait()

    ext_iota = lax.broadcasted_iota(jnp.int32, (EXT, ATOMS), 0)

    def build(group, first, cols):
        for u in range(group):
            slot = first + u
            row = nbr_ref[pl.ds(slot, 1), :]
            hot[:, pl.ds(pl.multiple_of(slot * ATOMS, ATOMS), ATOMS)] = jnp.where(
                ext_iota == row, 1.0, 0.0
            ).astype(bf16)

    over_slots(build, once)

    w8 = jnp.concatenate([win_ref[0], win_ref[1]], axis=1)
    w8_hi = w8.astype(bf16).astype(f32)
    w8_low = w8 - w8_hi
    win32[...] = jnp.zeros_like(win32)
    win32[0:8, :] = w8_hi
    win32[8:16, :] = w8_hi
    win32[16:24, :] = w8_low
    w_in_t = (0.5 * win32[...].T[:, :32]).astype(bf16)
    w_in_b = (0.5 * jnp.concatenate([w8_hi, w8_low], axis=0)).astype(bf16)
    small8[...] = jnp.zeros_like(small8)
    small8[0:2, :] = emb_ref[...]
    small8[2:3, :] = wen_ref[...]
    columns = small8[...].T
    light_col, heavy_col, energy_col = columns[:, 0:1], columns[:, 1:2], columns[:, 2:3]
    kinds = mm(small8[0:8, :].astype(bf16), wmsg_ref[0]).astype(bf16).astype(f32)
    w_out0 = wout_ref[0].astype(f32)
    pair_out = jnp.concatenate([w_out0 * kinds[0:1, :], w_out0 * kinds[1:2, :]], axis=0)
    pair_out_t = pair_out.T.astype(bf16)
    pair_buf[...] = pair_out.astype(bf16)
    w_upd0_t = wupd_ref[0].astype(f32).T.astype(bf16)
    scale = float(1.0 / np.sqrt(SLOTS))
    front = (mm(w_upd0_t, pair_out_t) * (0.5 * scale)).astype(bf16)

    a_right.wait_recv()
    a_left.wait_recv()
    row_g = lax.broadcasted_iota(jnp.int32, (8, 2 * FACES), 0)
    lane_g = lax.broadcasted_iota(jnp.int32, (8, 2 * FACES), 1)
    shift = jnp.where(row_g == 2, jnp.where(lane_g < FACES, -slab_width, slab_width), 0.0)
    ghost8 = jnp.where(lane_g < FACES, recv_a[0], recv_a[1]) + shift
    ext32[:, :ATOMS] = own32
    ext32[:, ATOMS:] = split_rows(ghost8)

    hsum[...] = jnp.zeros_like(hsum)

    def geometry(group, first, cols):
        rows = lax.broadcasted_iota(jnp.int32, (8, group * ATOMS), 0)
        orders = rows.astype(f32) + 1.0
        is_xyz = rows < 3
        found = join_rows(mm(ext32[...], hot[:, cols]))
        away = jnp.where(is_xyz, found - tile(own8, group), 0.0)
        square = jnp.sum(away * away, axis=0, keepdims=True) + soft_square
        inverse = lax.rsqrt(square)
        scaled = square * inverse * (1.0 / cutoff_radius)
        unit_buf[:, cols] = away * inverse
        phase = orders * scaled
        sign, z = turn(phase)
        rest = 1.0 - scaled * scaled
        ratio = rest * rest * inverse
        waves = sign * sin_pi(z, z * z) * ratio
        reach_buf[0:1, cols] = scaled
        reach_buf[1:2, cols] = inverse
        waves_hi = waves.astype(bf16).astype(f32)
        stack = jnp.concatenate(
            [waves_hi, waves - waves_hi, waves_hi, jnp.zeros_like(waves)], axis=0
        ).astype(bf16)
        basis_buf[:, cols] = stack
        act, slope = silu_of_half(mm(w_in_t[:HID], stack))
        d0_buf[:, cols] = slope.astype(bf16)
        with_heavy = found[3:4]
        with_light = found[4:5] - with_heavy
        mask_buf[0:1, cols] = with_light
        mask_buf[1:2, cols] = with_heavy
        hsum[0:HID, :] += fold(act * with_light)
        hsum[HID:, :] += fold(act * with_heavy)

    over_slots(geometry, once)

    act0, slope0 = silu_of_half(mm(front, hsum[...].astype(bf16)))
    layer_one = (jnp.where(heavy > 0.5, heavy_col, light_col) + act0).astype(bf16)
    send_b[...] = mm_nt(face_hot, layer_one).astype(bf16)
    b_right = halo(2, send_b.at[pl.ds(0, FACES)], recv_b.at[pl.ds(0, FACES)], right)
    b_left = halo(3, send_b.at[pl.ds(FACES, FACES)], recv_b.at[pl.ds(FACES, FACES)], left)
    b_right.start()
    b_left.start()
    q_copies = [to_bead(0, q_all, gap) for gap in range(1, beads)]
    for copy in q_copies:
        copy.start()
    w_out1 = wout_ref[1]
    held_one[...] = layer_one

    def late_weights(step, carry):
        w_out1_buf[...] = wout_ref[1].astype(f32).T.astype(bf16)
        w_upd1_buf[...] = wupd_ref[1].astype(f32).T.astype(bf16)
        w_msg1_t = wmsg_ref[1].astype(f32).T.astype(bf16)
        w_msg1_buf[...] = w_msg1_t
        source_buf[:, :ATOMS] = mm(w_msg1_t, held_one[...]).astype(bf16)
        back_buf[...] = (mm(pair_buf[...], wupd_ref[0]) * (0.25 * scale)).astype(bf16)
        return carry

    lax.fori_loop(0, once, late_weights, 0)
    is_heavy = jnp.where(
        lax.broadcasted_iota(jnp.int32, (8, CH), 0) < 4, heavy[:, :CH], heavy[:, CH:]
    )
    mass = jnp.where(is_heavy > 0.5, heavy_mass, light_mass)
    inverse_mass = jnp.where(is_heavy > 0.5, 1.0 / heavy_mass, 1.0 / light_mass)
    pos8[...] = jnp.zeros_like(pos8)
    for c in range(3):
        pos8[c : c + 1, :] = mom_ref[c]
    mom8 = pos8[...]

    def second_radial(group, first, cols):
        rows = lax.broadcasted_iota(jnp.int32, (8, group * ATOMS), 0)
        orders = rows.astype(f32) + 1.0
        scaled = reach_buf[0:1, cols]
        inverse = reach_buf[1:2, cols]
        sign, z = turn(orders * scaled)
        zz = z * z
        rest = 1.0 - scaled * scaled
        ratio = rest * rest * inverse
        ratio_slope = -(0.5 * scaled * rest + ratio) * inverse
        slope_buf[:, cols] = sign * (
            cos_pi(zz) * (orders * (ratio * (np.pi / cutoff_radius))) + sin_pi(z, zz) * ratio_slope
        )
        act, slope = silu_of_half(mm(w_in_t[HID:], basis_buf[:, cols]))
        d1_buf[:, cols] = slope.astype(bf16)
        rad_buf[:, cols] = mm(w_out1_buf[...], act.astype(bf16)).astype(bf16)

    over_slots(second_radial, once)

    b_right.wait_recv()
    b_left.wait_recv()
    source_buf[:, ATOMS:] = mm_nt(w_msg1_buf[...], recv_b[...]).astype(bf16)
    msum[...] = jnp.zeros_like(msum)

    def gather(group, first, cols):
        found = mm(source_buf[...], hot[:, cols])
        found = found.astype(bf16)
        gat_buf[:, cols] = found
        msum[...] += fold((found * rad_buf[:, cols]).astype(f32))

    over_slots(gather, once)

    msg1 = (msum[...] * (0.5 * scale)).astype(bf16)
    _, slope1 = silu_of_half(mm(w_upd1_buf[...], msg1))
    d_msg1 = (mm(wupd_ref[1], (energy_col * slope1).astype(bf16)) * (0.5 * scale)).astype(bf16)

    ghost_sum[...] = jnp.zeros_like(ghost_sum)

    def ghost_terms(group, first, cols):
        terms = rad_buf[:, cols] * tile(d_msg1, group)
        dt_buf[:, cols] = terms
        ghost_sum[...] += mm_nt(hot[ATOMS:, cols], terms)

    over_slots(ghost_terms, once)
    send_c[...] = ghost_sum[...].astype(bf16)
    c_left = halo(4, send_c.at[pl.ds(0, FACES)], recv_c.at[pl.ds(0, FACES)], left)
    c_right = halo(5, send_c.at[pl.ds(FACES, FACES)], recv_c.at[pl.ds(FACES, FACES)], right)
    c_left.start()
    c_right.start()

    msum[...] = jnp.zeros_like(msum)

    def own_terms(group, first, cols):
        msum[...] += mm_nt(dt_buf[:, cols], hot[:ATOMS, cols])
        d_rad = gat_buf[:, cols] * tile(d_msg1, group)
        d_pre = mm(w_out1, d_rad).astype(bf16) * d1_buf[:, cols]
        d_basis = mm(w_in_b[:, HID:], d_pre)
        db_buf[:, cols] = d_basis[0:8] + d_basis[8:16]

    over_slots(own_terms, once)
    d_one = mm(wmsg_ref[1], msum[...].astype(bf16)) + energy_col

    c_left.wait_recv()
    c_right.wait_recv()
    d_one += mm(mm_nt(wmsg_ref[1], recv_c[...]).astype(bf16), face_hot)
    d_hid0 = mm(back_buf[...], (d_one * (2.0 * slope0)).astype(bf16)).astype(bf16)
    d_light, d_heavy = d_hid0[:HID], d_hid0[HID:]

    msum[0:8, :] = jnp.zeros((8, ATOMS), f32)
    fghost[...] = jnp.zeros_like(fghost)

    def first_back(group, first, cols):
        with_light = mask_buf[0:1, cols].astype(bf16)
        with_heavy = mask_buf[1:2, cols].astype(bf16)
        d_act = tile(d_light, group) * with_light + tile(d_heavy, group) * with_heavy
        d_pre = d_act * d0_buf[:, cols]
        d_basis = mm(w_in_b[:, :HID], d_pre)
        d_basis = d_basis[0:8] + d_basis[8:16] + db_buf[:, cols]
        d_dist = jnp.sum(d_basis * slope_buf[:, cols], axis=0, keepdims=True)
        pull = unit_buf[:, cols] * d_dist
        msum[0:8, :] += fold(pull)
        pull_hi = pull.astype(bf16).astype(f32)
        pulls = jnp.concatenate([pull_hi, pull - pull_hi], axis=0).astype(bf16)
        f_buf[:, cols] = pulls
        fghost[...] += mm_nt(pulls, hot[ATOMS:, cols])

    over_slots(first_back, once)
    send_d[...] = fghost[0:8, :] + fghost[8:16, :]
    d_left = halo(6, send_d, recv_d.at[0], left)
    d_right = halo(7, send_d, recv_d.at[1], right)
    d_left.start()
    d_right.start()

    msum[16:32, :] = jnp.zeros((16, ATOMS), f32)

    def own_pulls(group, first, cols):
        msum[16:32, :] += mm_nt(f_buf[:, cols], hot[:ATOMS, cols])

    over_slots(own_pulls, once)
    force8 = msum[0:8, :] - msum[16:24, :] - msum[24:32, :]

    d_left.wait_recv()
    d_right.wait_recv()
    returned = jnp.where(lane_g < FACES, recv_d[0], recv_d[1])
    force8 = force8 - join_rows(mm(split_rows(returned), face_hot))

    kick8 = mom8 + (0.5 * time_step) * force8
    p_all[0] = kick8[:, :CH] + pltpu.roll(kick8[:, CH:], 4, 0)
    p_copies = [to_bead(1, p_all, gap) for gap in range(1, beads)]
    for copy in p_copies:
        copy.start()
    for c in range(3):
        out_ref[6 + c] = force8[c : c + 1]

    cosine, reach, pull = mode_mix(beads)
    for copy in q_copies:
        copy.wait_recv()
    new_q = jnp.zeros((8, CH), f32)
    new_p = jnp.zeros((8, CH), f32)
    for gap in range(beads):
        new_q += cosine[gap] * q_all[gap]
        new_p += pull[gap] * q_all[gap]
    new_p = new_p * mass
    for copy in p_copies:
        copy.wait_recv()
    from_p = jnp.zeros((8, CH), f32)
    for gap in range(beads):
        from_p += reach[gap] * p_all[gap]
        new_p += cosine[gap] * p_all[gap]
    new_q += from_p * inverse_mass
    for c in range(3):
        for half in range(2):
            row = c + 4 * half
            out_ref[c, :, half * CH : half * CH + CH] = new_q[row : row + 1]
            out_ref[3 + c, :, half * CH : half * CH + CH] = new_p[row : row + 1]

    for copy in (a_right, a_left, b_right, b_left, c_left, c_right, d_left, d_right):
        copy.wait_send()
    for copy in q_copies + p_copies:
        copy.wait_send()


def per_device(
    positions,
    momenta,
    species,
    neighbours,
    send_low,
    send_high,
    species_embed,
    w_radial_in,
    w_radial_out,
    w_message,
    w_update,
    w_energy,
):
    beads = lax.axis_size("bead")
    slabs = lax.axis_size("space")
    vmem = pl.BlockSpec(memory_space=pltpu.VMEM)
    result = pltpu.VMEM((9, 1, ATOMS), f32)
    piece = jax.ShapeDtypeStruct((3, 1, ATOMS), f32)
    moved = pl.pallas_call(
        functools.partial(kernel, beads, slabs),
        out_shape=result,
        in_specs=[pl.BlockSpec(memory_space=pltpu.HBM)] * 12,
        out_specs=vmem,
        scratch_shapes=[
            pltpu.VMEM((3, 1, ATOMS), f32),
            pltpu.VMEM((3, 1, ATOMS), f32),
            pltpu.VMEM((1, ATOMS), jnp.int32),
            pltpu.VMEM((SLOTS, ATOMS), jnp.int32),
            pltpu.VMEM((1, FACES), jnp.int32),
            pltpu.VMEM((1, FACES), jnp.int32),
            pltpu.VMEM((2, CH), f32),
            pltpu.VMEM((2, 8, HID), f32),
            pltpu.VMEM((2, HID, CH), bf16),
            pltpu.VMEM((2, CH, CH), bf16),
            pltpu.VMEM((2, CH, CH), bf16),
            pltpu.VMEM((1, CH), f32),
            pltpu.VMEM((8, ATOMS), f32),
            pltpu.VMEM((128, CH), f32),
            pltpu.VMEM((128, 2 * HID), f32),
            pltpu.VMEM((EXT, EDGES), bf16),
            pltpu.VMEM((32, EXT), bf16),
            pltpu.VMEM((32, EDGES), bf16),
            pltpu.VMEM((8, EDGES), f32),
            pltpu.VMEM((8, EDGES), f32),
            pltpu.VMEM((8, EDGES), f32),
            pltpu.VMEM((8, EDGES), f32),
            pltpu.VMEM((CH, ATOMS), bf16),
            pltpu.VMEM((CH, HID), bf16),
            pltpu.VMEM((CH, CH), bf16),
            pltpu.VMEM((CH, CH), bf16),
            pltpu.VMEM((CH, CH), bf16),
            pltpu.VMEM((CH, CH), bf16),
            pltpu.VMEM((CH, EXT), bf16),
            pltpu.VMEM((HID, EDGES), bf16),
            pltpu.VMEM((HID, EDGES), bf16),
            pltpu.VMEM((CH, EDGES), bf16),
            pltpu.VMEM((CH, EDGES), bf16),
            pltpu.VMEM((CH, EDGES), bf16),
            pltpu.VMEM((8, EDGES), f32),
            pltpu.VMEM((16, EDGES), bf16),
            pltpu.VMEM((2 * HID, ATOMS), f32),
            pltpu.VMEM((CH, ATOMS), f32),
            pltpu.VMEM((2 * FACES, CH), f32),
            pltpu.VMEM((16, 2 * FACES), f32),
            pltpu.VMEM((8, 2 * FACES), f32),
            pltpu.VMEM((2, 8, 2 * FACES), f32),
            pltpu.VMEM((2 * FACES, CH), bf16),
            pltpu.VMEM((2 * FACES, CH), bf16),
            pltpu.VMEM((2 * FACES, CH), bf16),
            pltpu.VMEM((2 * FACES, CH), bf16),
            pltpu.VMEM((8, 2 * FACES), f32),
            pltpu.VMEM((2, 8, 2 * FACES), f32),
            pltpu.VMEM((beads, 8, CH), f32),
            pltpu.VMEM((beads, 8, CH), f32),
            pltpu.SemaphoreType.DMA((8,)),
            pltpu.SemaphoreType.DMA((8,)),
            pltpu.SemaphoreType.DMA((2 * beads,)),
            pltpu.SemaphoreType.DMA((2 * beads,)),
            pltpu.SemaphoreType.DMA((12,)),
        ],
        compiler_params=pltpu.CompilerParams(
            collective_id=0, has_side_effects=True, vmem_limit_bytes=60 * 1024 * 1024
        ),
    )(
        jnp.transpose(positions, (1, 0, 2)),
        jnp.transpose(momenta, (1, 0, 2)),
        species.reshape(1, ATOMS),
        neighbours.T,
        send_low.reshape(1, FACES),
        send_high.reshape(1, FACES),
        species_embed,
        w_radial_in,
        w_radial_out,
        w_message,
        w_update,
        w_energy.reshape(1, CH),
    )
    outs = [moved[3 * n : 3 * n + 3] for n in range(3)]
    return tuple(jnp.transpose(out, (1, 0, 2)) for out in outs)


def solution(mesh):
    in_specs = (
        P("bead", None, "space"),
        P("bead", None, "space"),
        P("space"),
        P("space", None),
        P("space"),
        P("space"),
        P(),
        P(),
        P(),
        P(),
        P(),
        P(),
    )
    out_specs = (P("bead", None, "space"), P("bead", None, "space"), P("bead", None, "space"))
    return jax.shard_map(
        per_device, mesh=mesh, in_specs=in_specs, out_specs=out_specs, check_vma=False
    )
```

```python
import functools

import jax
import jax.numpy as jnp
import numpy as np
from jax import lax
from jax.experimental import pallas as pl
from jax.experimental.pallas import tpu as pltpu
from jax.sharding import PartitionSpec as P

cutoff_radius = 8.0
slab_width = 3.0
soft_square = 0.25
time_step = 0.5
cycle_angle = 2.0
light_mass = 1.0
heavy_mass = 16.0

ATOMS = 256
FACES = 64
SLOTS = 24
CH = 128
HID = 64
GROUPS = {
    "build": 8,
    "geometry": 24,
    "second_radial": 24,
    "gather": 24,
    "ghost_terms": 24,
    "own_terms": 24,
    "first_back": 24,
    "own_pulls": 8,
}
EDGES = SLOTS * ATOMS
EXT = ATOMS + 2 * FACES

f32 = jnp.float32
bf16 = jnp.bfloat16
NT = (((1,), (1,)), ((), ()))


def mm(a, b):
    return jnp.dot(a, b, preferred_element_type=f32)


def mm_nt(a, b):
    return lax.dot_general(a, b, NT, preferred_element_type=f32)


def split_rows(x):
    hi = x.astype(bf16).astype(f32)
    mid = (x - hi).astype(bf16).astype(f32)
    low = x - hi - mid
    return jnp.concatenate([hi, mid, low, jnp.zeros_like(x)], axis=0).astype(bf16)


def join_rows(y):
    return y[0:8] + y[8:16] + y[16:24]


def tile(a, group):
    return jnp.concatenate([a] * group, axis=1)


def fold(a):
    parts = [a[:, u * ATOMS : (u + 1) * ATOMS] for u in range(a.shape[1] // ATOMS)]
    while len(parts) > 1:
        pairs = [x + y for x, y in zip(parts[::2], parts[1::2])]
        parts = pairs + parts[2 * len(pairs) :]
    return parts[0]


def silu_of_half(y):
    t = jnp.tanh(y)
    u = y * t
    return y + u, (1.0 + t) * (1.0 + (y - u))


def over_slots(body, once):
    group = GROUPS[body.__name__]
    lanes = group * ATOMS

    def one(step, carry):
        body(group, step * group, pl.ds(pl.multiple_of(step * lanes, lanes), lanes))
        return carry

    lax.fori_loop(0, once if group == SLOTS else SLOTS // group, one, 0)


def sin_pi(z, zz):
    acc = -np.pi**11 / 39916800.0
    for c in (np.pi**9 / 362880.0, -np.pi**7 / 5040.0, np.pi**5 / 120.0, -np.pi**3 / 6.0, np.pi):
        acc = acc * zz + float(c)
    return acc * z


def turn(phase):
    whole = jnp.floor(phase + 0.5)
    return 1.0 - 2.0 * (whole - 2.0 * jnp.floor(whole * 0.5)), phase - whole


def cos_pi(zz):
    acc = np.pi**12 / 479001600.0
    for c in (
        -np.pi**10 / 3628800.0,
        np.pi**8 / 40320.0,
        -np.pi**6 / 720.0,
        np.pi**4 / 24.0,
        -np.pi**2 / 2.0,
        1.0,
    ):
        acc = acc * zz + float(c)
    return acc


def mode_mix(bead_count):
    k = np.arange(bead_count)
    angle = 2.0 * cycle_angle * np.sin(np.pi * k / bead_count)
    sinc = np.where(k > 0, np.sin(angle) / np.where(k > 0, angle, 1.0), 1.0)
    weights = (np.cos(angle), time_step * sinc, -angle * np.sin(angle) / time_step)
    gap = np.cos(2.0 * np.pi * k[:, None] * k[None, :] / bead_count) / bead_count
    return [[float(v) for v in gap @ w] for w in weights]


def kernel(
    beads,
    slabs,
    pos_hbm,
    mom_hbm,
    spec_hbm,
    nbr_hbm,
    low_hbm,
    high_hbm,
    emb_hbm,
    win_hbm,
    wout_hbm,
    wmsg_hbm,
    wupd_hbm,
    wen_hbm,
    out_ref,
    pos_ref,
    mom_ref,
    spec_ref,
    nbr_ref,
    low_ref,
    high_ref,
    emb_ref,
    win_ref,
    wout_ref,
    wmsg_ref,
    wupd_ref,
    wen_ref,
    pos8,
    small8,
    win32,
    hot,
    ext32,
    basis_buf,
    slope_buf,
    unit_buf,
    reach_buf,
    mask_buf,
    held_one,
    w_out1_buf,
    w_upd1_buf,
    w_msg1_buf,
    pair_buf,
    back_buf,
    source_buf,
    d0_buf,
    d1_buf,
    rad_buf,
    gat_buf,
    dt_buf,
    db_buf,
    f_buf,
    hsum,
    msum,
    ghost_sum,
    fghost,
    send_a,
    recv_a,
    send_b,
    recv_b,
    send_c,
    recv_c,
    send_d,
    recv_d,
    q_all,
    p_all,
    halo_send,
    halo_recv,
    bead_send,
    bead_recv,
    load_sem,
):
    bead = lax.axis_index("bead")
    slab = lax.axis_index("space")
    left = lax.rem(slab + slabs - 1, slabs)
    right = lax.rem(slab + 1, slabs)
    once = lax.div(slab + slabs, slabs)

    def halo(n, src, dst, target):
        return pltpu.make_async_remote_copy(
            src_ref=src,
            dst_ref=dst,
            send_sem=halo_send.at[n],
            recv_sem=halo_recv.at[n],
            device_id=(bead, target),
            device_id_type=pl.DeviceIdType.MESH,
        )

    def to_bead(n, buf, gap):
        return pltpu.make_async_remote_copy(
            src_ref=buf.at[0],
            dst_ref=buf.at[beads - gap],
            send_sem=bead_send.at[n * beads + gap],
            recv_sem=bead_recv.at[n * beads + beads - gap],
            device_id=(lax.rem(bead + gap, beads), slab),
            device_id_type=pl.DeviceIdType.MESH,
        )

    sources_hbm = (
        pos_hbm,
        spec_hbm,
        low_hbm,
        high_hbm,
        nbr_hbm,
        emb_hbm,
        win_hbm,
        wout_hbm,
        wmsg_hbm,
        wupd_hbm,
        wen_hbm,
        mom_hbm,
    )
    targets = (
        pos_ref,
        spec_ref,
        low_ref,
        high_ref,
        nbr_ref,
        emb_ref,
        win_ref,
        wout_ref,
        wmsg_ref,
        wupd_ref,
        wen_ref,
        mom_ref,
    )
    loads = [
        pltpu.make_async_copy(src, dst, load_sem.at[n])
        for n, (src, dst) in enumerate(zip(sources_hbm, targets))
    ]
    for load in loads[:4]:
        load.start()

    barrier = pltpu.get_barrier_semaphore()
    for target in (left, right):
        pl.semaphore_signal(
            barrier, inc=1, device_id=(bead, target), device_id_type=pl.DeviceIdType.MESH
        )
    for gap in range(1, beads):
        pl.semaphore_signal(
            barrier,
            inc=1,
            device_id=(lax.rem(bead + gap, beads), slab),
            device_id_type=pl.DeviceIdType.MESH,
        )

    for load in loads[4:]:
        load.start()
    for load in loads[:4]:
        load.wait()

    heavy = (spec_ref[...] == 1).astype(f32)
    pos8[...] = jnp.zeros_like(pos8)
    for c in range(3):
        pos8[c : c + 1, :] = pos_ref[c]
    own8 = pos8[...]
    q_all[0] = own8[:, :CH] + pltpu.roll(own8[:, CH:], 4, 0)
    row8 = lax.broadcasted_iota(jnp.int32, (8, ATOMS), 0)
    code8 = own8 + jnp.where(row8 == 3, heavy, 0.0) + jnp.where(row8 == 4, 1.0, 0.0)

    face_row = jnp.concatenate([high_ref[...], low_ref[...]], axis=1)
    face_t = jnp.where(
        lax.broadcasted_iota(jnp.int32, (ATOMS, 2 * FACES), 0) == face_row, 1.0, 0.0
    )
    face_hot_t = face_t.astype(bf16)
    face_hot = face_t.T.astype(bf16)
    own32 = split_rows(code8)
    send_a[...] = join_rows(mm(own32, face_hot_t))

    pl.semaphore_wait(barrier, beads + 1)
    a_right = halo(0, send_a, recv_a.at[0], right)
    a_left = halo(1, send_a, recv_a.at[1], left)
    a_right.start()
    a_left.start()

    for load in loads[4:]:
        load.wait()

    ext_iota = lax.broadcasted_iota(jnp.int32, (EXT, ATOMS), 0)

    def build(group, first, cols):
        for u in range(group):
            slot = first + u
            row = nbr_ref[pl.ds(slot, 1), :]
            hot[:, pl.ds(pl.multiple_of(slot * ATOMS, ATOMS), ATOMS)] = jnp.where(
                ext_iota == row, 1.0, 0.0
            ).astype(bf16)

    over_slots(build, once)

    w8 = jnp.concatenate([win_ref[0], win_ref[1]], axis=1)
    w8_hi = w8.astype(bf16).astype(f32)
    w8_low = w8 - w8_hi
    win32[...] = jnp.zeros_like(win32)
    win32[0:8, :] = w8_hi
    win32[8:16, :] = w8_hi
    win32[16:24, :] = w8_low
    w_in_t = (0.5 * win32[...].T[:, :32]).astype(bf16)
    w_in_b = (0.5 * jnp.concatenate([w8_hi, w8_low], axis=0)).astype(bf16)
    small8[...] = jnp.zeros_like(small8)
    small8[0:2, :] = emb_ref[...]
    small8[2:3, :] = wen_ref[...]
    columns = small8[...].T
    light_col, heavy_col, energy_col = columns[:, 0:1], columns[:, 1:2], columns[:, 2:3]
    kinds = mm(small8[0:8, :].astype(bf16), wmsg_ref[0]).astype(bf16).astype(f32)
    w_out0 = wout_ref[0].astype(f32)
    pair_out = jnp.concatenate([w_out0 * kinds[0:1, :], w_out0 * kinds[1:2, :]], axis=0)
    pair_out_t = pair_out.T.astype(bf16)
    pair_buf[...] = pair_out.astype(bf16)
    w_upd0_t = wupd_ref[0].astype(f32).T.astype(bf16)
    scale = float(1.0 / np.sqrt(SLOTS))
    front = (mm(w_upd0_t, pair_out_t) * (0.5 * scale)).astype(bf16)

    a_right.wait_recv()
    a_left.wait_recv()
    row_g = lax.broadcasted_iota(jnp.int32, (8, 2 * FACES), 0)
    lane_g = lax.broadcasted_iota(jnp.int32, (8, 2 * FACES), 1)
    shift = jnp.where(row_g == 2, jnp.where(lane_g < FACES, -slab_width, slab_width), 0.0)
    ghost8 = jnp.where(lane_g < FACES, recv_a[0], recv_a[1]) + shift
    ext32[:, :ATOMS] = own32
    ext32[:, ATOMS:] = split_rows(ghost8)

    hsum[...] = jnp.zeros_like(hsum)

    def geometry(group, first, cols):
        rows = lax.broadcasted_iota(jnp.int32, (8, group * ATOMS), 0)
        orders = rows.astype(f32) + 1.0
        is_xyz = rows < 3
        found = join_rows(mm(ext32[...], hot[:, cols]))
        away = jnp.where(is_xyz, found - tile(own8, group), 0.0)
        square = jnp.sum(away * away, axis=0, keepdims=True) + soft_square
        inverse = lax.rsqrt(square)
        scaled = square * inverse * (1.0 / cutoff_radius)
        unit_buf[:, cols] = away * inverse
        phase = orders * scaled
        sign, z = turn(phase)
        rest = 1.0 - scaled * scaled
        ratio = rest * rest * inverse
        waves = sign * sin_pi(z, z * z) * ratio
        reach_buf[0:1, cols] = scaled
        reach_buf[1:2, cols] = inverse
        waves_hi = waves.astype(bf16).astype(f32)
        stack = jnp.concatenate(
            [waves_hi, waves - waves_hi, waves_hi, jnp.zeros_like(waves)], axis=0
        ).astype(bf16)
        basis_buf[:, cols] = stack
        act, slope = silu_of_half(mm(w_in_t[:HID], stack))
        d0_buf[:, cols] = slope.astype(bf16)
        with_heavy = found[3:4]
        with_light = found[4:5] - with_heavy
        mask_buf[0:1, cols] = with_light
        mask_buf[1:2, cols] = with_heavy
        hsum[0:HID, :] += fold(act * with_light)
        hsum[HID:, :] += fold(act * with_heavy)

    over_slots(geometry, once)

    act0, slope0 = silu_of_half(mm(front, hsum[...].astype(bf16)))
    layer_one = (jnp.where(heavy > 0.5, heavy_col, light_col) + act0).astype(bf16)
    send_b[...] = mm_nt(face_hot, layer_one).astype(bf16)
    b_right = halo(2, send_b.at[pl.ds(0, FACES)], recv_b.at[pl.ds(0, FACES)], right)
    b_left = halo(3, send_b.at[pl.ds(FACES, FACES)], recv_b.at[pl.ds(FACES, FACES)], left)
    b_right.start()
    b_left.start()
    w_out1 = wout_ref[1]
    held_one[...] = layer_one

    def late_weights(step, carry):
        w_out1_buf[...] = wout_ref[1].astype(f32).T.astype(bf16)
        w_upd1_buf[...] = wupd_ref[1].astype(f32).T.astype(bf16)
        w_msg1_t = wmsg_ref[1].astype(f32).T.astype(bf16)
        w_msg1_buf[...] = w_msg1_t
        source_buf[:, :ATOMS] = mm(w_msg1_t, held_one[...]).astype(bf16)
        back_buf[...] = (mm(pair_buf[...], wupd_ref[0]) * (0.25 * scale)).astype(bf16)
        return carry

    lax.fori_loop(0, once, late_weights, 0)
    is_heavy = jnp.where(
        lax.broadcasted_iota(jnp.int32, (8, CH), 0) < 4, heavy[:, :CH], heavy[:, CH:]
    )
    mass = jnp.where(is_heavy > 0.5, heavy_mass, light_mass)
    inverse_mass = jnp.where(is_heavy > 0.5, 1.0 / heavy_mass, 1.0 / light_mass)
    pos8[...] = jnp.zeros_like(pos8)
    for c in range(3):
        pos8[c : c + 1, :] = mom_ref[c]
    mom8 = pos8[...]

    def second_radial(group, first, cols):
        rows = lax.broadcasted_iota(jnp.int32, (8, group * ATOMS), 0)
        orders = rows.astype(f32) + 1.0
        scaled = reach_buf[0:1, cols]
        inverse = reach_buf[1:2, cols]
        sign, z = turn(orders * scaled)
        zz = z * z
        rest = 1.0 - scaled * scaled
        ratio = rest * rest * inverse
        ratio_slope = -(0.5 * scaled * rest + ratio) * inverse
        slope_buf[:, cols] = sign * (
            cos_pi(zz) * (orders * (ratio * (np.pi / cutoff_radius))) + sin_pi(z, zz) * ratio_slope
        )
        act, slope = silu_of_half(mm(w_in_t[HID:], basis_buf[:, cols]))
        d1_buf[:, cols] = slope.astype(bf16)
        rad_buf[:, cols] = mm(w_out1_buf[...], act.astype(bf16)).astype(bf16)

    over_slots(second_radial, once)

    b_right.wait_recv()
    b_left.wait_recv()
    source_buf[:, ATOMS:] = mm_nt(w_msg1_buf[...], recv_b[...]).astype(bf16)
    msum[...] = jnp.zeros_like(msum)

    def gather(group, first, cols):
        found = mm(source_buf[...], hot[:, cols])
        gat_buf[:, cols] = found.astype(bf16)
        msum[...] += fold(found * rad_buf[:, cols].astype(f32))

    over_slots(gather, once)

    msg1 = (msum[...] * (0.5 * scale)).astype(bf16)
    _, slope1 = silu_of_half(mm(w_upd1_buf[...], msg1))
    d_msg1 = (mm(wupd_ref[1], (energy_col * slope1).astype(bf16)) * (0.5 * scale)).astype(bf16)

    ghost_sum[...] = jnp.zeros_like(ghost_sum)

    def ghost_terms(group, first, cols):
        terms = rad_buf[:, cols] * tile(d_msg1, group)
        dt_buf[:, cols] = terms
        ghost_sum[...] += mm_nt(hot[ATOMS:, cols], terms)

    over_slots(ghost_terms, once)
    send_c[...] = ghost_sum[...].astype(bf16)
    c_left = halo(4, send_c.at[pl.ds(0, FACES)], recv_c.at[pl.ds(0, FACES)], left)
    c_right = halo(5, send_c.at[pl.ds(FACES, FACES)], recv_c.at[pl.ds(FACES, FACES)], right)
    c_left.start()
    c_right.start()

    msum[...] = jnp.zeros_like(msum)

    def own_terms(group, first, cols):
        msum[...] += mm_nt(dt_buf[:, cols], hot[:ATOMS, cols])
        d_rad = gat_buf[:, cols] * tile(d_msg1, group)
        d_pre = mm(w_out1, d_rad).astype(bf16) * d1_buf[:, cols]
        d_basis = mm(w_in_b[:, HID:], d_pre)
        db_buf[:, cols] = d_basis[0:8] + d_basis[8:16]

    over_slots(own_terms, once)
    d_one = mm(wmsg_ref[1], msum[...].astype(bf16)) + energy_col

    c_left.wait_recv()
    c_right.wait_recv()
    d_one += mm(mm_nt(wmsg_ref[1], recv_c[...]).astype(bf16), face_hot)
    d_hid0 = mm(back_buf[...], (d_one * (2.0 * slope0)).astype(bf16)).astype(bf16)
    d_light, d_heavy = d_hid0[:HID], d_hid0[HID:]

    msum[0:8, :] = jnp.zeros((8, ATOMS), f32)
    fghost[...] = jnp.zeros_like(fghost)

    def first_back(group, first, cols):
        with_light = mask_buf[0:1, cols].astype(bf16)
        with_heavy = mask_buf[1:2, cols].astype(bf16)
        d_act = tile(d_light, group) * with_light + tile(d_heavy, group) * with_heavy
        d_pre = d_act * d0_buf[:, cols]
        d_basis = mm(w_in_b[:, :HID], d_pre)
        d_basis = d_basis[0:8] + d_basis[8:16] + db_buf[:, cols]
        d_dist = jnp.sum(d_basis * slope_buf[:, cols], axis=0, keepdims=True)
        pull = unit_buf[:, cols] * d_dist
        msum[0:8, :] += fold(pull)
        pull_hi = pull.astype(bf16).astype(f32)
        pulls = jnp.concatenate([pull_hi, pull - pull_hi], axis=0).astype(bf16)
        f_buf[:, cols] = pulls
        fghost[...] += mm_nt(pulls, hot[ATOMS:, cols])

    over_slots(first_back, once)
    send_d[...] = fghost[0:8, :] + fghost[8:16, :]
    d_left = halo(6, send_d, recv_d.at[0], left)
    d_right = halo(7, send_d, recv_d.at[1], right)
    d_left.start()
    d_right.start()
    q_copies = [to_bead(0, q_all, gap) for gap in range(1, beads)]
    for copy in q_copies:
        copy.start()

    msum[16:32, :] = jnp.zeros((16, ATOMS), f32)

    def own_pulls(group, first, cols):
        msum[16:32, :] += mm_nt(f_buf[:, cols], hot[:ATOMS, cols])

    over_slots(own_pulls, once)
    force8 = msum[0:8, :] - msum[16:24, :] - msum[24:32, :]

    d_left.wait_recv()
    d_right.wait_recv()
    returned = jnp.where(lane_g < FACES, recv_d[0], recv_d[1])
    force8 = force8 - join_rows(mm(split_rows(returned), face_hot))

    kick8 = mom8 + (0.5 * time_step) * force8
    p_all[0] = kick8[:, :CH] + pltpu.roll(kick8[:, CH:], 4, 0)
    p_copies = [to_bead(1, p_all, gap) for gap in range(1, beads)]
    for copy in p_copies:
        copy.start()
    for c in range(3):
        out_ref[6 + c] = force8[c : c + 1]

    cosine, reach, pull = mode_mix(beads)
    for copy in q_copies:
        copy.wait_recv()
    new_q = jnp.zeros((8, CH), f32)
    new_p = jnp.zeros((8, CH), f32)
    for gap in range(beads):
        new_q += cosine[gap] * q_all[gap]
        new_p += pull[gap] * q_all[gap]
    new_p = new_p * mass
    for copy in p_copies:
        copy.wait_recv()
    from_p = jnp.zeros((8, CH), f32)
    for gap in range(beads):
        from_p += reach[gap] * p_all[gap]
        new_p += cosine[gap] * p_all[gap]
    new_q += from_p * inverse_mass
    for c in range(3):
        for half in range(2):
            row = c + 4 * half
            out_ref[c, :, half * CH : half * CH + CH] = new_q[row : row + 1]
            out_ref[3 + c, :, half * CH : half * CH + CH] = new_p[row : row + 1]

    for copy in (a_right, a_left, b_right, b_left, c_left, c_right, d_left, d_right):
        copy.wait_send()
    for copy in q_copies + p_copies:
        copy.wait_send()


def per_device(
    positions,
    momenta,
    species,
    neighbours,
    send_low,
    send_high,
    species_embed,
    w_radial_in,
    w_radial_out,
    w_message,
    w_update,
    w_energy,
):
    beads = lax.axis_size("bead")
    slabs = lax.axis_size("space")
    vmem = pl.BlockSpec(memory_space=pltpu.VMEM)
    result = pltpu.VMEM((9, 1, ATOMS), f32)
    piece = jax.ShapeDtypeStruct((3, 1, ATOMS), f32)
    moved = pl.pallas_call(
        functools.partial(kernel, beads, slabs),
        out_shape=result,
        in_specs=[pl.BlockSpec(memory_space=pltpu.HBM)] * 12,
        out_specs=vmem,
        scratch_shapes=[
            pltpu.VMEM((3, 1, ATOMS), f32),
            pltpu.VMEM((3, 1, ATOMS), f32),
            pltpu.VMEM((1, ATOMS), jnp.int32),
            pltpu.VMEM((SLOTS, ATOMS), jnp.int32),
            pltpu.VMEM((1, FACES), jnp.int32),
            pltpu.VMEM((1, FACES), jnp.int32),
            pltpu.VMEM((2, CH), f32),
            pltpu.VMEM((2, 8, HID), f32),
            pltpu.VMEM((2, HID, CH), bf16),
            pltpu.VMEM((2, CH, CH), bf16),
            pltpu.VMEM((2, CH, CH), bf16),
            pltpu.VMEM((1, CH), f32),
            pltpu.VMEM((8, ATOMS), f32),
            pltpu.VMEM((128, CH), f32),
            pltpu.VMEM((128, 2 * HID), f32),
            pltpu.VMEM((EXT, EDGES), bf16),
            pltpu.VMEM((32, EXT), bf16),
            pltpu.VMEM((32, EDGES), bf16),
            pltpu.VMEM((8, EDGES), f32),
            pltpu.VMEM((8, EDGES), f32),
            pltpu.VMEM((8, EDGES), f32),
            pltpu.VMEM((8, EDGES), f32),
            pltpu.VMEM((CH, ATOMS), bf16),
            pltpu.VMEM((CH, HID), bf16),
            pltpu.VMEM((CH, CH), bf16),
            pltpu.VMEM((CH, CH), bf16),
            pltpu.VMEM((CH, CH), bf16),
            pltpu.VMEM((CH, CH), bf16),
            pltpu.VMEM((CH, EXT), bf16),
            pltpu.VMEM((HID, EDGES), bf16),
            pltpu.VMEM((HID, EDGES), bf16),
            pltpu.VMEM((CH, EDGES), bf16),
            pltpu.VMEM((CH, EDGES), bf16),
            pltpu.VMEM((CH, EDGES), bf16),
            pltpu.VMEM((8, EDGES), f32),
            pltpu.VMEM((16, EDGES), bf16),
            pltpu.VMEM((2 * HID, ATOMS), f32),
            pltpu.VMEM((CH, ATOMS), f32),
            pltpu.VMEM((2 * FACES, CH), f32),
            pltpu.VMEM((16, 2 * FACES), f32),
            pltpu.VMEM((8, 2 * FACES), f32),
            pltpu.VMEM((2, 8, 2 * FACES), f32),
            pltpu.VMEM((2 * FACES, CH), bf16),
            pltpu.VMEM((2 * FACES, CH), bf16),
            pltpu.VMEM((2 * FACES, CH), bf16),
            pltpu.VMEM((2 * FACES, CH), bf16),
            pltpu.VMEM((8, 2 * FACES), f32),
            pltpu.VMEM((2, 8, 2 * FACES), f32),
            pltpu.VMEM((beads, 8, CH), f32),
            pltpu.VMEM((beads, 8, CH), f32),
            pltpu.SemaphoreType.DMA((8,)),
            pltpu.SemaphoreType.DMA((8,)),
            pltpu.SemaphoreType.DMA((2 * beads,)),
            pltpu.SemaphoreType.DMA((2 * beads,)),
            pltpu.SemaphoreType.DMA((12,)),
        ],
        compiler_params=pltpu.CompilerParams(
            collective_id=0, has_side_effects=True, vmem_limit_bytes=60 * 1024 * 1024
        ),
    )(
        jnp.transpose(positions, (1, 0, 2)),
        jnp.transpose(momenta, (1, 0, 2)),
        species.reshape(1, ATOMS),
        neighbours.T,
        send_low.reshape(1, FACES),
        send_high.reshape(1, FACES),
        species_embed,
        w_radial_in,
        w_radial_out,
        w_message,
        w_update,
        w_energy.reshape(1, CH),
    )
    outs = [moved[3 * n : 3 * n + 3] for n in range(3)]
    return tuple(jnp.transpose(out, (1, 0, 2)) for out in outs)


def solution(mesh):
    in_specs = (
        P("bead", None, "space"),
        P("bead", None, "space"),
        P("space"),
        P("space", None),
        P("space"),
        P("space"),
        P(),
        P(),
        P(),
        P(),
        P(),
        P(),
    )
    out_specs = (P("bead", None, "space"), P("bead", None, "space"), P("bead", None, "space"))
    return jax.shard_map(
        per_device, mesh=mesh, in_specs=in_specs, out_specs=out_specs, check_vma=False
    )
```
